256 devices in a mesh: cube: 4 (over y_hi, core), row: 8 (over x, y_lo), col: 8 (over z).
Axes of the slice: x: 4, y: 4 (y_hi: 2, y_lo: 2; y = y_hi * 2 + y_lo), z: 8, core: 2. Of those that a mesh axis runs over, the one named last changes fastest.
Arguments:
- child_fronts: bfloat16 [4, 32, 128, 8, 8, 128], P(None, ('cube', 'row'), None, None, 'col'), as said below
- root_front: bfloat16 [4, 32, 128, 16, 8, 128], P(None, ('cube', 'row'), None, None, 'col'), as said below
- child_pivots: float32 [2, 10, 128, 128], replicated, as said below
- root_pivots: float32 [4, 128, 128], replicated, as said below
- child_maps: int32 [2, 54], replicated, may hold values from 10 to 127, as said below
Outputs:
- child_factor: bfloat16 [4, 32, 128, 1280], P(None, ('cube', 'row'))
- root_factor: bfloat16 [4, 32, 128, 512], P(None, ('cube', 'row'))
- root_rest: bfloat16 [4, 32, 128, 16, 8, 128], P(None, ('cube', 'row'), None, None, 'col')
The draws below stay inside these ranges and needn't reach their ends.
Inputs may be any that keep to these rules, and one draw needn't show every extreme that they name: `child_maps`: entry [c, a] is the root tile row that receives update tile row a of child c; each row of the list strictly increases, and entry [c, a] is congruent to a + 10 modulo 32. `child_fronts`: each child front, read as in the reference program, is symmetric. `root_front`: the root front, read as in the reference program, is symmetric. `child_pivots`: each block is zero below its diagonal. `root_pivots`: each block is zero below its diagonal.
All inputs are finite; a program needn't handle non-finite values.
Results may differ from the reference program's by a relative error of at most 0.0034.
Values may be sent and summed in bfloat16 or wider, within the bound.
A program may use at most 64 MiB of HBM per device.

```python
import jax
import jax.numpy as jnp
from jax import lax

B = 128
NC = 8192
NP = 16384
PANP = 4
PANC = 10
CHILD_ROWS = 16
GRID_ROWS = 32
GRID_COLS = 8
ALIGN = 32
CTR = 4
CTC = 8
RTR = 4
RTC = 16
UT = 54
SHIFTS = 2


def symmetric_front(key, order, diag_low, diag_high):
    keys = jax.random.split(key, 2)
    base_draw = jnp.clip(jax.random.normal(keys[0], (order, order), jnp.float32), -5.0, 5.0)
    matrix = (base_draw + base_draw.T) * 0.7071
    boost = jax.random.uniform(keys[1], (order,), jnp.float32, diag_low, diag_high)
    matrix = matrix + jnp.diag(boost)
    return matrix


def pivot_blocks(key, leading):
    keys = jax.random.split(key, 2)
    full_shape = leading + (B, B)
    diag_vals = jnp.exp(jax.random.uniform(keys[0], leading + (B,), jnp.float32, -0.35, 0.35))
    upper_vals = jnp.clip(jax.random.normal(keys[1], full_shape, jnp.float32), -5.0, 5.0)
    above = jnp.arange(B)[:, None] < jnp.arange(B)[None, :]
    diagonal = jnp.arange(B)[:, None] == jnp.arange(B)[None, :]
    return jnp.where(above, upper_vals * (0.72 / B), 0.0) + jnp.where(diagonal, diag_vals[..., None] * (0.2 / B) ** 0.5, 0.0)


def draw_child_fronts(key, part):
    keys = jax.random.split(key, 2)
    blocks_list = []
    for child_index in range(2):
        matrix = symmetric_front(keys[child_index], NC, 3.0, 5.0)
        blocks_list.append(matrix.reshape(CTR, CHILD_ROWS, B, CTC, GRID_COLS, B))
    return jnp.concatenate(blocks_list, axis=1).astype(jnp.bfloat16)


def draw_root_front(key, part):
    matrix = symmetric_front(jax.random.fold_in(key, 7), NP, 3.0, 5.0)
    return matrix.reshape(RTR, GRID_ROWS, B, RTC, GRID_COLS, B).astype(jnp.bfloat16)


def draw_child_pivots(key, part):
    return pivot_blocks(jax.random.fold_in(key, 11), (2, PANC))


def draw_root_pivots(key, part):
    return pivot_blocks(jax.random.fold_in(key, 13), (PANP,))


def draw_child_maps(key, part):
    picks = jax.random.randint(jax.random.fold_in(key, 17), (2, UT), 0, UT)
    rises = (picks < 2 * SHIFTS).astype(jnp.int32)
    rises = rises.at[:, 0].set(0)
    climbs = jnp.minimum(jnp.cumsum(rises, axis=1), SHIFTS)
    climbs = climbs.at[:, UT - 1].set(SHIFTS)
    base_rows = jnp.arange(UT, dtype=jnp.int32)[None, :] + PANC
    return (base_rows + ALIGN * climbs).astype(jnp.int32)


def setup_inputs(seed: int = 0) -> dict:
    splits = jax.random.split(jax.random.key(seed), 6)
    return {
        "child_fronts": draw_child_fronts(jax.random.fold_in(splits[5], 71), 0),
        "root_front": draw_root_front(jax.random.fold_in(splits[5], 71), 0),
        "child_pivots": draw_child_pivots(jax.random.fold_in(splits[5], 71), 0),
        "root_pivots": draw_root_pivots(jax.random.fold_in(splits[5], 71), 0),
        "child_maps": draw_child_maps(jax.random.fold_in(splits[5], 71), 0),
    }


def natural_child(child_fronts, child_index):
    child_block = child_fronts[:, child_index * CHILD_ROWS:(child_index + 1) * CHILD_ROWS]
    return child_block.reshape(NC, NC).astype(jnp.float32)


def eliminate(working, pivots, panel_count):
    row_ids = jnp.arange(working.shape[0], dtype=jnp.int32)
    panels = []
    for panel_step in range(panel_count):
        column = working[:, panel_step * B:(panel_step + 1) * B]
        factor = jnp.dot(column, pivots[panel_step], precision=lax.Precision.HIGHEST, preferred_element_type=jnp.float32)
        factor = jnp.where((row_ids >= panel_step * B)[:, None], factor, 0.0).astype(jnp.bfloat16)
        widened = factor.astype(jnp.float32)
        working = working - jnp.dot(widened, widened.T, precision=lax.Precision.HIGHEST, preferred_element_type=jnp.float32)
        panels.append(factor)
    return working, jnp.concatenate(panels, axis=1)


def reference(child_fronts, root_front, child_pivots, root_pivots, child_maps):
    root_matrix = root_front.reshape(NP // B, B, NP // B, B).astype(jnp.float32)
    child_panels = []
    for child_index in range(2):
        working, panels = eliminate(natural_child(child_fronts, child_index), child_pivots[child_index], PANC)
        rounded = lax.optimization_barrier(working[PANC * B:, PANC * B:].astype(jnp.bfloat16)).astype(jnp.float32)
        tiles_four = rounded.reshape(UT, B, UT, B).transpose(0, 2, 1, 3)
        targets = child_maps[child_index].astype(jnp.int32)
        root_matrix = root_matrix.at[targets[:, None], :, targets[None, :], :].add(tiles_four)
        child_panels.append(panels.reshape(CTR, CHILD_ROWS, B, PANC * B))
    root_matrix = root_matrix.reshape(NP, NP)
    root_matrix, root_panels = eliminate(root_matrix, root_pivots, PANP)
    child_factor = jnp.concatenate(child_panels, axis=1)
    root_factor = root_panels.reshape(RTR, GRID_ROWS, B, PANP * B)
    root_rest = root_matrix.astype(jnp.bfloat16).reshape(RTR, GRID_ROWS, B, RTC, GRID_COLS, B)
    return (child_factor, root_factor, root_rest)
```

```python
import functools

import jax
import jax.numpy as jnp
from jax import lax
from jax.experimental import pallas as pl
from jax.experimental.pallas import tpu as pltpu
from jax.sharding import PartitionSpec as P

B = 128
KC = 10
KR = 4
CS = 7
RS = 16
MESH = pl.DeviceIdType.MESH
BF = jnp.bfloat16
F32 = jnp.float32


def dot_nn(left, right):
    return lax.dot_general(left, right, (((1,), (0,)), ((), ())), preferred_element_type=F32)


def dot_nt(left, right):
    return lax.dot_general(left, right, (((1,), (1,)), ((), ())), preferred_element_type=F32)


def split(value):
    high = value.astype(BF)
    return high, (value - high.astype(F32)).astype(BF)


def times_pivot(value, pivot):
    high, low = split(value)
    pivot_high, pivot_low = split(pivot)
    return dot_nn(high, pivot_high) + (dot_nn(high, pivot_low) + dot_nn(low, pivot_high))


def pivot_times(pivot_t, value):
    high, low = split(value)
    pivot_high, pivot_low = split(pivot_t)
    return dot_nn(pivot_high, high) + (dot_nn(pivot_high, low) + dot_nn(pivot_low, high))


def position():
    cube = lax.axis_index("cube")
    return cube // 2, cube % 2, lax.axis_index("row"), lax.axis_index("col")


def gather_kernel(
    colt, rowt, rcolt, rrowt, top, down, side, rtop, rdown, rside,
    local_sem, tz_send, tz_recv, tp_send, tp_recv, rp_send, rp_recv, ring_send, ring_recv,
    rtz_send, rtz_recv, rtp_send, rtp_recv, rrp_send, rrp_recv, rring_send, rring_recv, sib_send,
):
    child, half, row, col = position()
    cube = lax.axis_index("cube")
    mine = half * 8 + row
    sibling = (child * 2 + 1 - half, row, col)
    barrier = pltpu.get_barrier_semaphore()

    def greet_line(step, carry):
        pl.semaphore_signal(
            barrier, inc=1, device_id=(cube, row, (col + step) % 8), device_id_type=MESH
        )
        return carry

    def greet_plane(step, carry):
        place = (cube * 8 + row + step) % 32
        pl.semaphore_signal(
            barrier, inc=1, device_id=(place // 8, place % 8, col), device_id_type=MESH
        )
        return carry

    lax.fori_loop(1, 8, greet_line, 0)
    lax.fori_loop(1, 32, greet_plane, 0)
    pl.semaphore_wait(barrier, 38)

    def remote(source, target, send, recv, device):
        return pltpu.make_async_remote_copy(
            src_ref=source, dst_ref=target, send_sem=send, recv_sem=recv,
            device_id=device, device_id_type=MESH,
        )

    def landed(ref, recv):
        remote(ref, ref, sib_send.at[0], recv, sibling).wait_recv()

    locals_ = []

    def local(cond, source, target):
        copy = pltpu.make_async_copy(source, target, local_sem.at[len(locals_)])
        locals_.append((cond, copy))
        pl.when(cond)(copy.start)

    owns = mine < KC
    rowner = (cube == 0) & (row < KR)
    for extra in range(2):
        index = col + 8 * extra
        cond = owns & (index <= mine) & (index < KC)
        local(cond, colt.at[extra, pl.ds(0, B)], top.at[mine % KC, index % KC])

        @pl.when(cond)
        def _():
            def send(step, carry):
                remote(
                    colt.at[extra, pl.ds(0, B)], top.at[mine % KC, index % KC],
                    tz_send.at[extra * 8 + step], tz_recv.at[index % KC],
                    (cube, row, (col + step) % 8),
                ).start()
                return carry

            lax.fori_loop(1, 8, send, 0)

    rcond = rowner & (col <= row) & (col < KR)
    local(rcond, rcolt.at[pl.ds(0, B)], rtop.at[row % KR, col % KR])

    @pl.when(rcond)
    def _():
        def send(step, carry):
            remote(
                rcolt.at[pl.ds(0, B)], rtop.at[row % KR, col % KR],
                rtz_send.at[step], rtz_recv.at[col % KR], (cube, row, (col + step) % 8),
            ).start()
            return carry

        lax.fori_loop(1, 8, send, 0)

    right = (cube, row, (col + 1) % 8)
    left = (cube, row, (col + 7) % 8)
    sends = []

    def ring(cond, source, buffer, slot, send, recv, device):
        copy = remote(source, buffer.at[slot], send, recv.at[slot], device)
        sends.append((cond, copy))
        pl.when(cond)(copy.start)

    always = col >= 0
    local(always, colt.at[0], down.at[col])
    local(col < 2, colt.at[1], down.at[8 + col % 2])
    local(col < KR, rcolt, rdown.at[col % KR])
    for way, device in ((0, right), (1, left)):
        ring(always, colt.at[0], down, col, ring_send.at[way], ring_recv, device)
        ring(col < 2, colt.at[1], down, 8 + col % 2, ring_send.at[8 + way], ring_recv, device)

    for i in range(KC):
        @pl.when(owns & (mine == i))
        def _():
            for index in range(i + 1):
                @pl.when(index % 8 != col)
                def _():
                    landed(top.at[i, index], tz_recv.at[index])

            block = top.at[i, pl.ds(0, i + 1)]
            for extra in range(2):
                @pl.when((col + 8 * extra <= i))
                def _():
                    locals_[extra][1].wait()

            def send(step, carry):
                remote(
                    block, block, tp_send.at[step], tp_recv.at[i],
                    (child * 2 + i % 2, (row + step) % 8, col),
                ).start()
                return carry

            lax.fori_loop(1, 8, send, 0)
            remote(block, block, tp_send.at[0], tp_recv.at[i], sibling).start()

    local(owns, rowt, side.at[mine % KC])

    @pl.when(owns)
    def _():
        target = side.at[mine % KC]

        def send(step, carry):
            remote(
                rowt, target, rp_send.at[step], rp_recv.at[mine % KC],
                (child * 2 + mine % 2, (row + step) % 8, col),
            ).start()
            return carry

        lax.fori_loop(1, 8, send, 0)
        remote(rowt, target, rp_send.at[0], rp_recv.at[mine % KC], sibling).start()

    def ring_step(step):
        for way, device in ((0, right), (1, left)):
            slot = (col + (8 - step if way == 0 else step)) % 8
            last = 4 if way == 0 else 3
            if step > last:
                continue
            landed(down.at[slot], ring_recv.at[slot])
            if step < last:
                ring(always, down.at[slot], down, slot, ring_send.at[step * 2 + way], ring_recv, device)
            more = slot < 2
            slot2 = 8 + slot % 2

            @pl.when(more)
            def _():
                landed(down.at[slot2], ring_recv.at[slot2])

            if step < last:
                ring(more, down.at[slot2], down, slot2, ring_send.at[8 + step * 2 + way], ring_recv, device)

    def root_step(step):
        for way, device in ((0, right), (1, left)):
            slot = (col + (8 - step if way == 0 else step)) % 8
            last = 4 if way == 0 else 3
            if step > last:
                continue
            more = slot < KR
            if step > 0:
                @pl.when(more)
                def _():
                    landed(rdown.at[slot % KR], rring_recv.at[slot % KR])
            if step < last:
                source = rcolt if step == 0 else rdown.at[slot % KR]
                ring(more, source, rdown, slot % KR, rring_send.at[step * 2 + way], rring_recv, device)

    def spread(buffer, slot, block, recv, index):
        here = (row != index % 8) | (half != index // 8)
        onward = (row != index % 8) & (half == slot % 2)

        @pl.when(here)
        def _():
            landed(block, recv.at[slot])

        copy = remote(block, block, sib_send.at[buffer * KC + slot], recv.at[slot], sibling)
        sends.append((onward, copy))
        pl.when(onward)(copy.start)

    ring_step(1)
    ring_step(2)
    for i in range(KC):
        spread(0, i, top.at[i, pl.ds(0, i + 1)], tp_recv, i)
    ring_step(3)
    ring_step(4)
    for i in range(KR):
        @pl.when(rowner & (row == i))
        def _():
            for index in range(i + 1):
                @pl.when(index != col)
                def _():
                    landed(rtop.at[i, index], rtz_recv.at[index])

            @pl.when(col <= i)
            def _():
                locals_[2][1].wait()

            block = rtop.at[i, pl.ds(0, i + 1)]

            def send(step, carry):
                place = (row + step) % 16
                device = (place // 8 * 2 + i % 2, place % 8, col)
                remote(block, block, rtp_send.at[step], rtp_recv.at[i], device).start()
                remote(rrowt, rside.at[i], rrp_send.at[step], rrp_recv.at[i], device).start()
                return carry

            lax.fori_loop(1, 16, send, 0)
            remote(block, block, rtp_send.at[0], rtp_recv.at[i], sibling).start()
            remote(rrowt, rside.at[i], rrp_send.at[0], rrp_recv.at[i], sibling).start()

    local(rowner, rrowt, rside.at[row % KR])
    for i in range(KC):
        spread(1, i, side.at[i], rp_recv, i)
    for step in range(5):
        root_step(step)

    def root_spread(kind, i, block, recv):
        same_chip = (child == 0) & (row == i)
        here = jnp.logical_not(same_chip & (half == 0))
        onward = jnp.logical_not(same_chip) & (half == i % 2)

        @pl.when(here)
        def _():
            landed(block, recv.at[i])

        copy = remote(block, block, sib_send.at[(2 + kind) * KC + i], recv.at[i], sibling)
        sends.append((onward, copy))
        pl.when(onward)(copy.start)

    for i in range(KR):
        root_spread(0, i, rtop.at[i, pl.ds(0, i + 1)], rtp_recv)
    for i in range(KR):
        root_spread(1, i, rside.at[i], rrp_recv)

    for number, (cond, copy) in enumerate(locals_):
        if number > 2:
            pl.when(cond)(copy.wait)
    for cond, copy in sends:
        pl.when(cond)(copy.wait_send)
    for extra in range(2):
        index = col + 8 * extra

        @pl.when(owns & (index <= mine) & (index < KC))
        def _():
            def drain(step, carry):
                remote(
                    colt.at[extra, pl.ds(0, B)], top.at[mine % KC, index % KC],
                    tz_send.at[extra * 8 + step], tz_recv.at[index % KC], sibling,
                ).wait_send()
                return carry

            lax.fori_loop(1, 8, drain, 0)

    @pl.when(rcond)
    def _():
        def drain(step, carry):
            remote(
                rcolt.at[pl.ds(0, B)], rtop.at[row % KR, col % KR],
                rtz_send.at[step], rtz_recv.at[0], sibling,
            ).wait_send()
            return carry

        lax.fori_loop(1, 8, drain, 0)

    for i in range(KC):
        @pl.when(owns & (mine == i))
        def _():
            block = top.at[i, pl.ds(0, i + 1)]

            def drain(step, carry):
                remote(block, block, tp_send.at[step], tp_recv.at[i], sibling).wait_send()
                remote(rowt, side.at[i], rp_send.at[step], rp_recv.at[i], sibling).wait_send()
                return carry

            lax.fori_loop(0, 8, drain, 0)

    for i in range(KR):
        @pl.when(rowner & (row == i))
        def _():
            block = rtop.at[i, pl.ds(0, i + 1)]

            def drain(step, carry):
                remote(block, block, rtp_send.at[step], rtp_recv.at[i], sibling).wait_send()
                remote(rrowt, rside.at[i], rrp_send.at[step], rrp_recv.at[i], sibling).wait_send()
                return carry

            lax.fori_loop(0, 16, drain, 0)


def gather(colt, rowt, rcolt, rrowt):
    dma = pltpu.SemaphoreType.DMA
    shapes = [
        (KC, KC, B, B), (KC, 4 * B, B), (KC, B, CS * B),
        (KR, KR, B, B), (KR, 4 * B, B), (KR, B, RS * B),
    ]
    return pl.pallas_call(
        gather_kernel,
        out_shape=[jax.ShapeDtypeStruct(shape, BF) for shape in shapes],
        in_specs=[pl.BlockSpec(memory_space=pl.ANY)] * 4,
        out_specs=[pl.BlockSpec(memory_space=pl.ANY)] * 6,
        scratch_shapes=[
            dma((8,)), dma((16,)), dma((KC,)), dma((8,)), dma((KC,)), dma((8,)), dma((KC,)),
            dma((16,)), dma((KC,)),
            dma((8,)), dma((KR,)), dma((16,)), dma((KR,)), dma((16,)), dma((KR,)), dma((8,)), dma((KR,)),
            dma((4 * KC,)),
        ],
        compiler_params=pltpu.CompilerParams(collective_id=0, has_side_effects=True),
    )(colt, rowt, rcolt, rrowt)


def factor(count, top, down, side, pivots, panels_top, panels, wide, row_class, first_tile):
    rows = panels.shape[0]
    columns = wide.shape[1]
    row_block = lax.broadcasted_iota(jnp.int32, (rows, B), 0) < B
    col_block = lax.broadcasted_iota(jnp.int32, (B, columns), 1) < B
    for pair in range(count // 2):
        k = 2 * pair
        at = k * B
        here, there = slice(at, at + B), slice(at + B, at + 2 * B)
        pivot, pivot2 = pivots[k], pivots[k + 1]
        pivot_t, pivot2_t = pivot.T, pivot2.T
        length = (count - k) * B
        first = top[k:count, k].reshape(length, B).astype(F32)
        second = top[k + 1:count, k + 1].reshape(length - B, B).astype(F32)
        own = down[k].astype(F32)
        own2 = down[k + 1].astype(F32)
        across = side[k].astype(F32)
        across2 = side[k + 1].astype(F32)
        if pair:
            lead = panels_top[at:at + 2 * B, :at]
            both = dot_nt(panels_top[at:, :at], lead)
            first = first - both[:, :B]
            second = second - both[B:, B:]
            both = dot_nt(panels[:, :at], lead)
            own = own - both[:, :B]
            own2 = own2 - both[:, B:]
            both = dot_nn(lead, wide[:at, :])
            across = across - both[:B]
            across2 = across2 - both[B:]
        first = times_pivot(first, pivot).astype(BF)
        panels_top[at:, here] = first
        link = first[B:2 * B]
        second = times_pivot(second - dot_nt(first[B:], link), pivot2).astype(BF)
        panels_top[at + B:, there] = second
        own = times_pivot(own, pivot)
        own = jnp.where(row_block & (row_class < k), 0.0, own).astype(BF)
        panels[:, here] = own
        own2 = times_pivot(own2 - dot_nt(own, link), pivot2)
        own2 = jnp.where(row_block & (row_class < k + 1), 0.0, own2).astype(BF)
        panels[:, there] = own2
        across = pivot_times(pivot_t, across)
        across = jnp.where(col_block & (first_tile < k), 0.0, across).astype(BF)
        wide[here, :] = across
        across2 = pivot_times(pivot2_t, across2 - dot_nn(link, across))
        across2 = jnp.where(col_block & (first_tile < k + 1), 0.0, across2).astype(BF)
        wide[there, :] = across2


def child_kernel(top, down, side, pivots, front, panels_out, keep, away, panels_top, wide, update):
    child, half, row, col = position()
    factor(KC, top, down, side, pivots, panels_top, panels_out, wide, half * 8 + row, 8 + col)
    for t in range(4):
        block = slice(t * B, (t + 1) * B)
        value = front[block, :].astype(F32) - dot_nn(panels_out[block, :], wide[...])
        update[t] = value.astype(BF)
    for p in range(2):
        keep[p] = update[2 * p + child]
        away[p] = update[2 * p + 1 - child]


def child_step(top, down, side, pivots, front):
    vmem = pl.BlockSpec(memory_space=pltpu.VMEM)
    return pl.pallas_call(
        child_kernel,
        out_shape=[
            jax.ShapeDtypeStruct((4 * B, KC * B), BF),
            jax.ShapeDtypeStruct((2, B, CS * B), BF),
            jax.ShapeDtypeStruct((2, B, CS * B), BF),
        ],
        in_specs=[vmem] * 5,
        out_specs=[vmem] * 3,
        scratch_shapes=[
            pltpu.VMEM((KC * B, KC * B), BF),
            pltpu.VMEM((KC * B, CS * B), BF),
            pltpu.VMEM((4, B, CS * B), BF),
        ],
        compiler_params=pltpu.CompilerParams(vmem_limit_bytes=48 * 2**20),
        cost_estimate=pl.CostEstimate(flops=8 * 10**9, bytes_accessed=10**7, transcendentals=0),
    )(top, down, side, pivots, front)


def root_kernel(top, down, side, pivots, front, panels_out, rest, panels_top, wide):
    child, half, row, col = position()
    factor(KR, top, down, side, pivots, panels_top, panels_out, wide, (child * 2 + half) * 8 + row, col)
    for t in range(4):
        block = slice(t * B, (t + 1) * B)
        rest[block, :] = front[block, :].astype(F32) - dot_nn(panels_out[block, :], wide[...])


def root_step(top, down, side, pivots, front):
    vmem = pl.BlockSpec(memory_space=pltpu.VMEM)
    return pl.pallas_call(
        root_kernel,
        out_shape=[
            jax.ShapeDtypeStruct((4 * B, KR * B), BF),
            jax.ShapeDtypeStruct((4 * B, RS * B), F32),
        ],
        in_specs=[vmem] * 5,
        out_specs=[vmem] * 2,
        scratch_shapes=[pltpu.VMEM((KR * B, KR * B), BF), pltpu.VMEM((KR * B, RS * B), BF)],
        compiler_params=pltpu.CompilerParams(vmem_limit_bytes=48 * 2**20),
        cost_estimate=pl.CostEstimate(flops=3 * 10**9, bytes_accessed=10**7, transcendentals=0),
    )(top, down, side, pivots, front)


def add_kernel(maps, rest, keep, came, out, total):
    child, half, row, col = position()
    total[...] = rest[...]
    for source, tiles in ((child, keep), (1 - child, came)):
        for p in range(2):
            i = (2 * p + child) * 16 + half * 8 + row - KC
            for s in range(1, 8):
                j = s * 8 + col - KC

                @pl.when((i >= 0) & (j >= 0))
                def _():
                    down = maps[source, jnp.maximum(i, 0)] // 32
                    across = maps[source, jnp.maximum(j, 0)] // 8
                    at = (pl.ds(pl.multiple_of(down * B, B), B), pl.ds(pl.multiple_of(across * B, B), B))
                    total[at] += tiles[p, :, (s - 1) * B:s * B].astype(F32)
    for t in range(4):
        for b in range(0, B, 32):
            value = total[t * B + b:t * B + b + 32, :].reshape(32, RS, B)
            out[t, b:b + 32] = value.astype(BF)


def add_step(maps, rest, keep, came):
    vmem = pl.BlockSpec(memory_space=pltpu.VMEM)
    return pl.pallas_call(
        add_kernel,
        out_shape=jax.ShapeDtypeStruct((4, B, RS, B), BF),
        in_specs=[pl.BlockSpec(memory_space=pltpu.SMEM)] + [vmem] * 3,
        out_specs=vmem,
        scratch_shapes=[pltpu.VMEM((4 * B, RS * B), F32)],
        compiler_params=pltpu.CompilerParams(vmem_limit_bytes=48 * 2**20),
    )(maps, rest, keep, came)


def on_device(child_fronts, root_front, child_pivots, root_pivots, child_maps):
    child = lax.axis_index("cube") // 2
    fronts = child_fronts.reshape(4, B, 8, B)
    roots = root_front.reshape(4, B, RS, B)
    colt = fronts[:, :, :2, :].transpose(2, 0, 1, 3).reshape(2, 4 * B, B)
    rowt = fronts[0, :, 1:, :].reshape(B, CS * B)
    rcolt = roots[:, :, 0, :].reshape(4 * B, B)
    rrowt = roots[0].reshape(B, RS * B)
    front = fronts[:, :, 1:, :].reshape(4 * B, CS * B)
    root = roots.reshape(4 * B, RS * B)
    top, down, side, rtop, rdown, rside = gather(colt, rowt, rcolt, rrowt)
    pivots = lax.dynamic_index_in_dim(child_pivots, child, 0, keepdims=False)
    panels, keep, away = child_step(top, down, side, pivots, front)
    pairs = [(source, source ^ 2) for source in range(4)]
    came = lax.ppermute(away, "cube", pairs)
    root_panels, rest = root_step(rtop, rdown, rside, root_pivots, root)
    root_rest = add_step(child_maps, rest, keep, came)
    return (
        panels.reshape(4, 1, B, KC * B),
        root_panels.reshape(4, 1, B, KR * B),
        root_rest.reshape(4, 1, B, RS, 1, B),
    )


def solution(mesh):
    placed = (
        P(None, ("cube", "row"), None, None, "col", None),
        P(None, ("cube", "row"), None, None, "col", None),
        P(),
        P(),
        P(),
    )
    return jax.shard_map(
        on_device,
        mesh=mesh,
        in_specs=placed,
        out_specs=(
            P(None, ("cube", "row"), None, None),
            P(None, ("cube", "row"), None, None),
            P(None, ("cube", "row"), None, None, "col", None),
        ),
        check_vma=False,
    )
```

```python
import functools

import jax
import jax.numpy as jnp
from jax import lax
from jax.experimental import pallas as pl
from jax.experimental.pallas import tpu as pltpu
from jax.sharding import PartitionSpec as P

B = 128
KC = 10
KR = 4
CS = 7
RS = 16
MESH = pl.DeviceIdType.MESH
BF = jnp.bfloat16
F32 = jnp.float32


def dot_nn(left, right):
    return lax.dot_general(left, right, (((1,), (0,)), ((), ())), preferred_element_type=F32)


def dot_nt(left, right):
    return lax.dot_general(left, right, (((1,), (1,)), ((), ())), preferred_element_type=F32)


def split(value):
    high = value.astype(BF)
    return high, (value - high.astype(F32)).astype(BF)


def times_pivot(value, pivot):
    high, low = split(value)
    pivot_high, pivot_low = split(pivot)
    return dot_nn(high, pivot_high) + (dot_nn(high, pivot_low) + dot_nn(low, pivot_high))


def pivot_times(pivot_t, value):
    high, low = split(value)
    pivot_high, pivot_low = split(pivot_t)
    return dot_nn(pivot_high, high) + (dot_nn(pivot_high, low) + dot_nn(pivot_low, high))


def position():
    cube = lax.axis_index("cube")
    return cube // 2, cube % 2, lax.axis_index("row"), lax.axis_index("col")


def neighbours(which):
    child, half, row, col = position()
    x, y = row // 2, child * 2 + row % 2
    if which == "x":
        return [(child * 2 + half, (x + d) % 4 * 2 + row % 2, col) for d in (1, 3, 2)]
    if which == "pair":
        return [(child * 2 + half, row + 1 - 2 * (row % 2), col)]
    places = [(y + d) % 4 for d in (1, 3, 2)]
    return [(place // 2 * 2 + half, x * 2 + place % 2, col) for place in places]


class Traffic:
    def __init__(self):
        self.pending = []

    def send(self, cond, source, target, send_sem, recv_sem, device):
        copy = pltpu.make_async_remote_copy(
            src_ref=source, dst_ref=target, send_sem=send_sem, recv_sem=recv_sem,
            device_id=device, device_id_type=MESH,
        )
        pl.when(cond)(copy.start)
        self.pending.append((cond, copy))

    def landed(self, cond, block, recv_sem):
        child, half, row, col = position()
        copy = pltpu.make_async_remote_copy(
            src_ref=block, dst_ref=block, send_sem=recv_sem, recv_sem=recv_sem,
            device_id=(child * 2 + 1 - half, row, col), device_id_type=MESH,
        )
        pl.when(cond)(copy.wait_recv)

    def drain(self):
        for cond, copy in self.pending:
            pl.when(cond)(copy.wait_send)
        self.pending = []


class Spread:
    def __init__(self, traffic, blocks, recv, send, whole):
        self.traffic, self.blocks, self.recv, self.sems = traffic, blocks, recv, send
        child, half, row, col = position()
        self.half = half
        self.sibling = (child * 2 + 1 - half, row, col)
        x, yl = row // 2, row % 2
        self.along_x = neighbours("x")
        self.along_y = neighbours("y" if whole else "pair")
        self.roles = []
        for i in range(len(blocks)):
            same_x = x == i % 8 // 2
            same_y = yl == i % 2
            if whole:
                same_y = same_y & (child == 0)
            self.roles.append((same_x, same_y, half == i // 8))

    def _out(self, cond, i, part, devices, first):
        for n, device in enumerate(devices):
            block = self.blocks[i][part]
            self.traffic.send(cond, block, block, self.sems.at[i, first + n], self.recv.at[part, i], device)

    def _wait(self, cond, i, part):
        self.traffic.landed(cond, self.blocks[i][part], self.recv.at[part, i])

    def parts(self, i):
        return [part for part in range(2) if self.blocks[i][part] is not None]

    def begin(self, i, ready):
        same_x, same_y, core = self.roles[i]
        chip = same_x & same_y
        for part in self.parts(i):
            self._out(ready & chip & core, i, part, [self.sibling], 6 + part)
        for part in self.parts(i):
            taker = self.half == part
            self._wait(chip & jnp.logical_not(core) & taker, i, part)
            one, two = (self.along_x, self.along_y) if part == 0 else (self.along_y, self.along_x)
            self._out(chip & taker, i, part, one, 0)
            self._out(chip & taker, i, part, two, 3)

    def relay(self, i):
        same_x, same_y, core = self.roles[i]
        for part in self.parts(i):
            near = (same_y & jnp.logical_not(same_x)) if part == 0 else (same_x & jnp.logical_not(same_y))
            near = near & (self.half == part)
            self._wait(near, i, part)
            self._out(near, i, part, self.along_y if part == 0 else self.along_x, 0)
            self._out(near, i, part, [self.sibling], 6)

    def settle(self, i):
        same_x, same_y, core = self.roles[i]
        for part in self.parts(i):
            far = jnp.logical_not(same_y if part == 0 else same_x) & (self.half == part)
            self._wait(far, i, part)
            self._out(far, i, part, [self.sibling], 7)

    def finish(self, i):
        same_x, same_y, core = self.roles[i]
        owner = same_x & same_y & core
        for part in self.parts(i):
            self._wait(jnp.logical_not(owner) & (self.half != part), i, part)


class Line:
    def __init__(self, traffic, buffer, count, recv, send):
        self.traffic, self.buffer, self.count, self.recv, self.sems = traffic, buffer, count, recv, send
        child, half, row, col = position()
        self.col = col
        self.place = lambda d: (child * 2 + half, row, (col + d) % 8)

    def _slots(self, step):
        base = (self.col + step) % 8
        for extra in range((self.count + 7) // 8):
            limit = min(self.count - 8 * extra, 8)
            cond = base < limit
            yield extra, cond, 8 * extra + base % limit

    def begin(self):
        for extra, cond, slot in self._slots(0):
            for n, d in enumerate((1, 7, 2, 6)):
                block = self.buffer.at[slot]
                self.traffic.send(cond, block, block, self.sems.at[extra, n], self.recv.at[slot], self.place(d))

    def relay(self):
        for n, (step, goals) in enumerate(((6, (1, 2)), (2, (7,)))):
            for extra, cond, slot in self._slots(step):
                block = self.buffer.at[slot]
                self.traffic.landed(cond, block, self.recv.at[slot])
                for m, d in enumerate(goals):
                    self.traffic.send(
                        cond, block, block, self.sems.at[extra, 4 + 2 * n + m], self.recv.at[slot], self.place(d)
                    )

    def finish(self):
        for step in (7, 1, 5, 3, 4):
            for extra, cond, slot in self._slots(step):
                self.traffic.landed(cond, self.buffer.at[slot], self.recv.at[slot])


class TopLine:
    def __init__(self, traffic, count, buffer, recv, send, owns, mine):
        child, half, row, col = position()
        self.traffic, self.count, self.buffer, self.recv, self.sems = traffic, count, buffer, recv, send
        self.owns, self.mine, self.col = owns, mine % count, col
        self.place = lambda d: (child * 2 + half, row, (col + d) % 8)

    def begin(self):
        for extra in range((self.count + 7) // 8):
            limit = min(self.count - 8 * extra, 8)
            index = 8 * extra + self.col % limit
            cond = self.owns & (self.col < limit) & (index <= self.mine)
            block = self.buffer.at[self.mine, index]
            for n, d in enumerate((1, 7, 2, 6, 3, 5, 4)):
                self.traffic.send(cond, block, block, self.sems.at[extra, n], self.recv.at[index], self.place(d))

    def finish(self):
        for index in range(self.count):
            cond = self.owns & (index <= self.mine) & (self.col != index % 8)
            self.traffic.landed(cond, self.buffer.at[self.mine, index], self.recv.at[index])


def greet_all():
    child, half, row, col = position()
    cube = child * 2 + half
    barrier = pltpu.get_barrier_semaphore()

    def greet_line(step, carry):
        pl.semaphore_signal(
            barrier, inc=1, device_id=(cube, row, (col + step) % 8), device_id_type=MESH
        )
        return carry

    lax.fori_loop(1, 8, greet_line, 0)
    others = neighbours("x") + neighbours("y") + [(child * 2 + 1 - half, row, col)]
    for device in others:
        pl.semaphore_signal(barrier, inc=1, device_id=device, device_id_type=MESH)
    return barrier, 7 + len(others)


def halves_of_tiles(buffer, count):
    blocks = []
    for i in range(count):
        middle = (i + 2) // 2
        second = buffer.at[i, pl.ds(middle, i + 1 - middle)] if i + 1 > middle else None
        blocks.append((buffer.at[i, pl.ds(0, middle)], second))
    return blocks


def halves_of_rows(buffer, count):
    return [
        (buffer.at[i, pl.ds(0, B // 2)], buffer.at[i, pl.ds(B // 2, B // 2)]) for i in range(count)
    ]


def factor_top(count, pair, top, pivots, panels):
    k = 2 * pair
    at = k * B
    length = (count - k) * B
    first = top[k:count, k].reshape(length, B).astype(F32)
    second = top[k + 1:count, k + 1].reshape(length - B, B).astype(F32)
    if pair:
        both = dot_nt(panels[at:, :at], panels[at:at + 2 * B, :at])
        first = first - both[:, :B]
        second = second - both[B:, B:]
    first = times_pivot(first, pivots[k]).astype(BF)
    panels[at:, at:at + B] = first
    second = second - dot_nt(first[B:], first[B:2 * B])
    panels[at + B:, at + B:at + 2 * B] = times_pivot(second, pivots[k + 1]).astype(BF)


def factor_own(pair, down, pivots, panels_top, panels, row_class):
    k = 2 * pair
    at = k * B
    row_block = lax.broadcasted_iota(jnp.int32, (panels.shape[0], B), 0) < B
    first = down[k].astype(F32)
    second = down[k + 1].astype(F32)
    if pair:
        both = dot_nt(panels[:, :at], panels_top[at:at + 2 * B, :at])
        first = first - both[:, :B]
        second = second - both[:, B:]
    first = times_pivot(first, pivots[k])
    first = jnp.where(row_block & (row_class < k), 0.0, first).astype(BF)
    panels[:, at:at + B] = first
    second = second - dot_nt(first, panels_top[at + B:at + 2 * B, at:at + B])
    second = times_pivot(second, pivots[k + 1])
    second = jnp.where(row_block & (row_class < k + 1), 0.0, second).astype(BF)
    panels[:, at + B:at + 2 * B] = second


def factor_wide(pair, side, pivots, panels_top, wide, first_tile):
    k = 2 * pair
    at = k * B
    col_block = lax.broadcasted_iota(jnp.int32, (B, wide.shape[1]), 1) < B
    first = side[k].astype(F32)
    second = side[k + 1].astype(F32)
    if pair:
        both = dot_nn(panels_top[at:at + 2 * B, :at], wide[:at, :])
        first = first - both[:B]
        second = second - both[B:]
    first = pivot_times(pivots[k].T, first)
    first = jnp.where(col_block & (first_tile < k), 0.0, first).astype(BF)
    wide[at:at + B, :] = first
    second = second - dot_nn(panels_top[at + B:at + 2 * B, at:at + B], first)
    second = pivot_times(pivots[k + 1].T, second)
    second = jnp.where(col_block & (first_tile < k + 1), 0.0, second).astype(BF)
    wide[at + B:at + 2 * B, :] = second


def main_kernel(
    fronts, roots, child_pivots, root_pivots,
    panels_out, root_panels_out, rest_out, keep_out, came_out,
    craw, rraw, cwide, rwide, cpiv, rpiv,
    top, down, side, rtop, rdown, rside,
    ctop, cown, cside, xtop, xown, xside, update,
    load_sem, store_sem, tl_send, tl_recv, rtl_send, rtl_recv, line_send, line_recv, rline_send, rline_recv,
    t_send, t_recv, s_send, s_recv, rt_send, rt_recv, rs_send, rs_recv, u_send, u_recv,
):
    child, half, row, col = position()
    mine = half * 8 + row
    root_class = child * 16 + mine
    owns = mine < KC
    root_owns = (child == 0) & (half == 0) & (row < KR)

    loads = [
        pltpu.make_async_copy(fronts, craw, load_sem.at[0]),
        pltpu.make_async_copy(child_pivots.at[child], cpiv, load_sem.at[1]),
        pltpu.make_async_copy(roots, rraw, load_sem.at[2]),
        pltpu.make_async_copy(root_pivots, rpiv, load_sem.at[3]),
    ]
    for load in loads:
        load.start()
    barrier, count = greet_all()

    loads[0].wait()
    for t in range(4):
        cwide[t * 8 * B:(t + 1) * 8 * B, :] = craw[t].astype(F32).reshape(8 * B, B)
    column = cwide[pl.ds(0, 4 * B, stride=8), :].astype(BF)
    down[col] = column

    @pl.when(owns & (col <= mine))
    def _():
        top[mine % KC, col] = column[:B]

    @pl.when(col < 2)
    def _():
        column2 = cwide[pl.ds(1, 4 * B, stride=8), :].astype(BF)
        down[8 + col % 2] = column2

        @pl.when(owns & (8 + col <= mine))
        def _():
            top[mine % KC, 8 + col % 2] = column2[:B]

    @pl.when(owns)
    def _():
        for s in range(CS):
            side[mine % KC, :, s * B:(s + 1) * B] = cwide[pl.ds(s + 1, B, stride=8), :].astype(BF)

    loads[2].wait()
    for t in range(4):
        for b in range(0, B, 32):
            at = (t * B + b) * RS
            rwide[at:at + 32 * RS, :] = rraw[t, b:b + 32].astype(F32).reshape(32 * RS, B)

    @pl.when(col < KR)
    def _():
        root_column = rwide[pl.ds(0, 4 * B, stride=RS), :].astype(BF)
        rdown[col % KR] = root_column

        @pl.when(root_owns & (col <= row))
        def _():
            rtop[row % KR, col % KR] = root_column[:B]

    @pl.when(root_owns)
    def _():
        for s in range(RS):
            rside[row % KR, :, s * B:(s + 1) * B] = rwide[pl.ds(s, B, stride=RS), :].astype(BF)

    traffic = Traffic()
    top_line = TopLine(traffic, KC, top, tl_recv, tl_send, owns, mine)
    root_top_line = TopLine(traffic, KR, rtop, rtl_recv, rtl_send, root_owns, row)
    line = Line(traffic, down, KC, line_recv, line_send)
    root_line = Line(traffic, rdown, KR, rline_recv, rline_send)
    top_spread = Spread(traffic, halves_of_tiles(top, KC), t_recv, t_send, False)
    side_spread = Spread(traffic, halves_of_rows(side, KC), s_recv, s_send, False)
    root_top_spread = Spread(traffic, halves_of_tiles(rtop, KR), rt_recv, rt_send, True)
    root_side_spread = Spread(traffic, halves_of_rows(rside, KR), rs_recv, rs_send, True)
    always = col >= 0

    pl.semaphore_wait(barrier, count)
    top_line.begin()
    root_top_line.begin()
    line.begin()
    for i in range(KC):
        side_spread.begin(i, always)
    top_line.finish()
    for i in range(KC):
        top_spread.begin(i, always)
    for i in range(KC):
        top_spread.relay(i)
    for i in range(KC):
        side_spread.relay(i)
    for i in range(KC):
        top_spread.settle(i)
    line.relay()
    for i in range(KC):
        top_spread.finish(i)
    root_line.begin()
    root_top_line.finish()
    for i in range(KR):
        root_top_spread.begin(i, always)
    for i in range(KR):
        root_side_spread.begin(i, always)

    loads[1].wait()
    loads[3].wait()
    factor_top(KC, 0, top, cpiv, ctop)
    factor_top(KC, 1, top, cpiv, ctop)
    for i in range(KC):
        side_spread.settle(i)
    factor_top(KC, 2, top, cpiv, ctop)
    factor_top(KC, 3, top, cpiv, ctop)
    factor_top(KC, 4, top, cpiv, ctop)
    line.finish()
    for pair in range(KC // 2):
        factor_own(pair, down, cpiv, ctop, cown, mine)
    panels_store = pltpu.make_async_copy(cown, panels_out, store_sem.at[0])
    panels_store.start()
    root_line.relay()
    for i in range(KR):
        root_top_spread.relay(i)
    for i in range(KR):
        root_side_spread.relay(i)
    for i in range(KC):
        side_spread.finish(i)
    for pair in range(KC // 2):
        factor_wide(pair, side, cpiv, ctop, cside, 8 + col)

    def update_rows(t):
        rows = pl.ds(pl.multiple_of(t * B, B), B)
        product = dot_nn(cown[rows, :], cside[...])
        for s in range(CS):
            first = t * 8 * B + s + 1
            value = cwide[pl.ds(first, B, stride=8), :] - product[:, s * B:(s + 1) * B]
            update[t, :, s * B:(s + 1) * B] = value.astype(BF)

    partner = ((1 - child) * 2 + half, row, col)
    for p in range(2):
        t = 2 * p + 1 - child
        update_rows(t)
        traffic.send(always, update.at[t], came_out.at[p], u_send.at[p], u_recv.at[p], partner)
    keep_stores = []
    for p in range(2):
        t = 2 * p + child
        update_rows(t)
        keep_stores.append(pltpu.make_async_copy(update.at[t], keep_out.at[p], store_sem.at[1 + p]))
        keep_stores[-1].start()

    for i in range(KR):
        root_top_spread.settle(i)
    for i in range(KR):
        root_side_spread.settle(i)
    root_line.finish()
    for i in range(KR):
        root_top_spread.finish(i)
    for pair in range(KR // 2):
        factor_top(KR, pair, rtop, rpiv, xtop)
    for pair in range(KR // 2):
        factor_own(pair, rdown, rpiv, xtop, xown, root_class)
    root_panels_store = pltpu.make_async_copy(xown, root_panels_out, store_sem.at[3])
    root_panels_store.start()
    for i in range(KR):
        root_side_spread.finish(i)
    for pair in range(KR // 2):
        factor_wide(pair, rside, rpiv, xtop, xside, col)
    rest_stores = []
    for t in range(4):
        product = dot_nn(xown[t * B:(t + 1) * B, :], xside[...])
        for s in range(RS):
            place = pl.ds(t * RS * B + s, B, stride=RS)
            rwide[place, :] = rwide[place, :] - product[:, s * B:(s + 1) * B]
        block = pl.ds(t * RS * B, RS * B)
        rest_stores.append(pltpu.make_async_copy(rwide.at[block], rest_out.at[block], store_sem.at[4 + t]))
        rest_stores[-1].start()

    for p in range(2):
        traffic.landed(always, came_out.at[p], u_recv.at[p])
    traffic.drain()
    for store in [panels_store, root_panels_store] + keep_stores + rest_stores:
        store.wait()


def main_step(fronts, roots, child_pivots, root_pivots):
    dma = pltpu.SemaphoreType.DMA
    anywhere = pl.BlockSpec(memory_space=pl.ANY)
    return pl.pallas_call(
        main_kernel,
        out_shape=[
            jax.ShapeDtypeStruct((4 * B, KC * B), BF),
            jax.ShapeDtypeStruct((4 * B, KR * B), BF),
            jax.ShapeDtypeStruct((4 * B * RS, B), F32),
            jax.ShapeDtypeStruct((2, B, CS * B), BF),
            jax.ShapeDtypeStruct((2, B, CS * B), BF),
        ],
        in_specs=[anywhere] * 4,
        out_specs=[anywhere] * 5,
        scratch_shapes=[
            pltpu.VMEM((4, B, 8, B), BF),
            pltpu.VMEM((4, B, RS, B), BF),
            pltpu.VMEM((4 * B * 8, B), F32),
            pltpu.VMEM((4 * B * RS, B), F32),
            pltpu.VMEM((KC, B, B), F32),
            pltpu.VMEM((KR, B, B), F32),
            pltpu.VMEM((KC, KC, B, B), BF),
            pltpu.VMEM((KC, 4 * B, B), BF),
            pltpu.VMEM((KC, B, CS * B), BF),
            pltpu.VMEM((KR, KR, B, B), BF),
            pltpu.VMEM((KR, 4 * B, B), BF),
            pltpu.VMEM((KR, B, RS * B), BF),
            pltpu.VMEM((KC * B, KC * B), BF),
            pltpu.VMEM((4 * B, KC * B), BF),
            pltpu.VMEM((KC * B, CS * B), BF),
            pltpu.VMEM((KR * B, KR * B), BF),
            pltpu.VMEM((4 * B, KR * B), BF),
            pltpu.VMEM((KR * B, RS * B), BF),
            pltpu.VMEM((4, B, CS * B), BF),
            dma((4,)), dma((8,)),
            dma((2, 7)), dma((KC,)), dma((1, 7)), dma((KR,)),
            dma((2, 8)), dma((KC,)), dma((1, 8)), dma((KR,)),
            dma((KC, 8)), dma((2, KC)), dma((KC, 8)), dma((2, KC)),
            dma((KR, 8)), dma((2, KR)), dma((KR, 8)), dma((2, KR)),
            dma((2,)), dma((2,)),
        ],
        compiler_params=pltpu.CompilerParams(
            collective_id=0, has_side_effects=True, vmem_limit_bytes=56 * 2**20
        ),
        cost_estimate=pl.CostEstimate(flops=10**10, bytes_accessed=10**7, transcendentals=0),
    )(fronts, roots, child_pivots, root_pivots)


def add_kernel(maps, rest, keep, came, panels, root_panels, out, panels_out, root_panels_out, total, tiles, done, sems):
    child, half, row, col = position()
    passes = [
        pltpu.make_async_copy(panels, panels_out, sems.at[0]),
        pltpu.make_async_copy(root_panels, root_panels_out, sems.at[1]),
    ]
    fetch = [pltpu.make_async_copy(source, tiles.at[n], sems.at[2 + n]) for n, source in enumerate((keep, came))]
    height = RS * B
    blocks = [pl.ds(t * height, height) for t in range(4)]
    fetch += [pltpu.make_async_copy(rest.at[blocks[t]], total.at[blocks[t]], sems.at[4 + t]) for t in range(4)]
    for copy in fetch + passes:
        copy.start()
    for copy in fetch:
        copy.wait()
    for number, source in enumerate((child, 1 - child)):
        for p in range(2):
            i = (2 * p + child) * 16 + half * 8 + row - KC
            for s in range(1, 8):
                j = s * 8 + col - KC

                @pl.when((i >= 0) & (j >= 0))
                def _():
                    below = maps[source, jnp.maximum(i, 0)] // 32
                    across = maps[source, jnp.maximum(j, 0)] // 8
                    place = pl.ds(below * height + across, B, stride=RS)
                    total[place, :] = total[place, :] + tiles[number, p, :, (s - 1) * B:s * B].astype(F32)
    stores = []
    for t in range(4):
        for b in range(0, B, 32):
            at = (t * B + b) * RS
            done[t, b:b + 32] = total[at:at + 32 * RS, :].astype(BF).reshape(32, RS, B)
        stores.append(pltpu.make_async_copy(done.at[t], out.at[t], sems.at[8 + t]))
        stores[-1].start()
    for copy in stores + passes:
        copy.wait()


def add_step(maps, rest, keep, came, panels, root_panels):
    anywhere = pl.BlockSpec(memory_space=pl.ANY)
    return pl.pallas_call(
        add_kernel,
        out_shape=[
            jax.ShapeDtypeStruct((4, B, RS, B), BF),
            jax.ShapeDtypeStruct((4 * B, KC * B), BF),
            jax.ShapeDtypeStruct((4 * B, KR * B), BF),
        ],
        in_specs=[pl.BlockSpec(memory_space=pltpu.SMEM)] + [anywhere] * 5,
        out_specs=[anywhere] * 3,
        scratch_shapes=[
            pltpu.VMEM((4 * B * RS, B), F32),
            pltpu.VMEM((2, 2, B, CS * B), BF),
            pltpu.VMEM((4, B, RS, B), BF),
            pltpu.SemaphoreType.DMA((12,)),
        ],
        compiler_params=pltpu.CompilerParams(vmem_limit_bytes=48 * 2**20),
    )(maps, rest, keep, came, panels, root_panels)


def on_device(child_fronts, root_front, child_pivots, root_pivots, child_maps):
    fronts = child_fronts.reshape(4, B, 8, B)
    roots = root_front.reshape(4, B, RS, B)
    panels, root_panels, rest, keep, came = main_step(fronts, roots, child_pivots, root_pivots)
    root_rest, panels, root_panels = add_step(child_maps, rest, keep, came, panels, root_panels)
    return (
        panels.reshape(4, 1, B, KC * B),
        root_panels.reshape(4, 1, B, KR * B),
        root_rest.reshape(4, 1, B, RS, 1, B),
    )


def solution(mesh):
    placed = (
        P(None, ("cube", "row"), None, None, "col", None),
        P(None, ("cube", "row"), None, None, "col", None),
        P(),
        P(),
        P(),
    )
    return jax.shard_map(
        on_device,
        mesh=mesh,
        in_specs=placed,
        out_specs=(
            P(None, ("cube", "row"), None, None),
            P(None, ("cube", "row"), None, None),
            P(None, ("cube", "row"), None, None, "col", None),
        ),
        check_vma=False,
    )
```

```python
import functools

import jax
import jax.numpy as jnp
from jax import lax
from jax.experimental import pallas as pl
from jax.experimental.pallas import tpu as pltpu
from jax.sharding import PartitionSpec as P

B = 128
KC = 10
KR = 4
CS = 7
RS = 16
MESH = pl.DeviceIdType.MESH
BF = jnp.bfloat16
F32 = jnp.float32


def dot_nn(left, right):
    return lax.dot_general(left, right, (((1,), (0,)), ((), ())), preferred_element_type=F32)


def dot_nt(left, right):
    return lax.dot_general(left, right, (((1,), (1,)), ((), ())), preferred_element_type=F32)


def split(value):
    high = value.astype(BF)
    return high, (value - high.astype(F32)).astype(BF)


def times_pivot(value, pivot):
    pivot_high, pivot_low = split(pivot)
    upper = jnp.concatenate([pivot_high, pivot_low], axis=1)
    lower = jnp.concatenate([pivot_high, jnp.zeros_like(pivot_low)], axis=1)
    product = dot_nn(jnp.concatenate(split(value), axis=1), jnp.concatenate([upper, lower], axis=0))
    return product[:, :B] + product[:, B:]


def pivot_times(pivot_t, value):
    pivot_high, pivot_low = split(pivot_t)
    upper = jnp.concatenate([pivot_high, pivot_high], axis=1)
    lower = jnp.concatenate([pivot_low, jnp.zeros_like(pivot_low)], axis=1)
    product = dot_nn(jnp.concatenate([upper, lower], axis=0), jnp.concatenate(split(value), axis=0))
    return product[:B] + product[B:]


def position():
    cube = lax.axis_index("cube")
    return cube // 2, cube % 2, lax.axis_index("row"), lax.axis_index("col")


class Starter:
    def __init__(self, number=0):
        self.number = number

    def send(self, source, target, send_sem, recv_sem, device):
        remote(source, target, send_sem, recv_sem, device).start()

    def landed(self, block, recv_sem):
        child, half, row, col = position()
        remote(block, block, recv_sem, recv_sem, (child * 2 + 1 - half, row, col)).wait_recv()


class Drainer:
    def __init__(self, number=0):
        self.number = number

    def send(self, source, target, send_sem, recv_sem, device):
        remote(source, target, send_sem, recv_sem, device).wait_send()

    def landed(self, block, recv_sem):
        pass


def remote(source, target, send_sem, recv_sem, device):
    return pltpu.make_async_remote_copy(
        src_ref=source, dst_ref=target, send_sem=send_sem, recv_sem=recv_sem,
        device_id=device, device_id_type=MESH,
    )


class Traffic:
    def __init__(self):
        self.pending = []

    def starter(self):
        return Starter()

    def run(self, cond, body, number=0):
        op = Starter(number)
        pl.when(cond)(lambda: body(op))
        self.pending.append((cond, body, number))
        return op.number

    def drain(self):
        for cond, body, number in self.pending:
            pl.when(cond)(lambda: body(Drainer(number)))
        self.pending = []


class PairSpread:
    def __init__(self, traffic, buffer, size, hand, recv, sems):
        self.traffic, self.buffer, self.size, self.hand = traffic, buffer, size, hand
        self.recv, self.sems, self.number = recv, sems, 0
        child, half, row, col = position()
        self.half, self.row, self.x, self.y = half, row, row // 2, row % 2
        self.sibling = (child * 2 + 1 - half, row, col)
        self.plus, self.minus = [(child * 2 + half, (self.x + d) % 4 * 2 + self.y, col) for d in (1, 3)]
        self.across = (child * 2 + half, row + 1 - 2 * self.y, col)
        self.mine = half * 8 + row
        self.other = (1 - half) * 8 + row

    def part(self, slot, half):
        if self.size is None:
            return self.buffer.at[slot], self.recv.at[0, slot]
        start = pl.multiple_of(half * self.size, self.size)
        return self.buffer.at[slot, pl.ds(start, self.size)], self.recv.at[half, slot]

    def _send(self, op, slot, device, half=None):
        block, recv = self.part(slot, self.half if half is None else half)
        op.send(block, block, self.sems.at[op.number], recv, device)
        op.number += 1

    def _wait(self, op, slot, half=None):
        block, recv = self.part(slot, self.half if half is None else half)
        op.landed(block, recv)

    def _pass(self, op, slot):
        if self.size is not None:
            self._send(op, slot, self.sibling)

    def _run(self, cond, body):
        self.number = self.traffic.run(cond, body, self.number)

    def _each(self, chips, body):
        for chip in chips:
            body(chip)
            pl.when(chip < 2)(lambda: body(8 + chip % 2))

    def _row(self, d, e):
        return (self.x + d) % 4 * 2 + (self.y + e) % 2

    def begin(self):
        def own(op):
            slot = self.mine % KC
            if self.size is None:
                block, recv = self.part(slot, self.half)
                op.send(self.hand, block, self.sems.at[op.number], recv, self.sibling)
                op.number += 1
            else:
                self._send(op, slot, self.sibling, 1 - self.half)
            for device in (self.across, self.plus, self.minus):
                self._send(op, slot, device)
            self._pass(op, slot)

        def others(op):
            slot = self.other % KC
            self._wait(op, slot)
            for device in (self.across, self.plus, self.minus):
                self._send(op, slot, device)

        self._run(self.mine < KC, own)
        self._run(self.other < KC, others)

    def _onward(self, op, slot, d):
        if d == 3:
            pl.when(slot < 4)(lambda: self._send(op, slot, self.plus))
        else:
            pl.when(slot >= 4)(lambda: self._send(op, slot, self.minus))

    def relay(self):
        def first(op):
            for d in (3, 1):
                def body(slot):
                    self._wait(op, slot)
                    self._onward(op, slot, d)
                    self._send(op, slot, self.across)
                    self._pass(op, slot)

                self._each([self._row(d, 0)], body)

        def second(op):
            def body(slot):
                self._wait(op, slot)
                self._send(op, slot, self.plus)
                self._send(op, slot, self.minus)
                self._pass(op, slot)

            self._each([self._row(0, 1)], body)

        self._run(self.half == 0, first)
        self._run(self.half == 1, second)

    def relay2(self):
        def first(op):
            def body(slot):
                self._wait(op, slot)
                self._send(op, slot, self.across)
                self._pass(op, slot)

            self._each([self._row(2, 0)], body)

        def second(op):
            for e in range(2):
                for d in (3, 1):
                    def body(slot):
                        self._wait(op, slot)
                        self._onward(op, slot, d)
                        self._pass(op, slot)

                    self._each([self._row(d, e)], body)

        self._run(self.half == 0, first)
        self._run(self.half == 1, second)

    def settle(self):
        def body(op, slot):
            self._wait(op, slot)
            self._pass(op, slot)

        def first(op):
            self._each([self._row(d, 1) for d in (0, 3, 1, 2)], lambda slot: body(op, slot))

        def second(op):
            self._each([self._row(2, e) for e in range(2)], lambda slot: body(op, slot))

        self._run(self.half == 0, first)
        self._run(self.half == 1, second)

    def finish(self):
        if self.size is None:
            return
        op = self.traffic.starter()
        pl.when(self.other < KC)(lambda: self._wait(op, self.other % KC, 1 - self.half))
        chips = [self._row(d, e) for d in range(4) for e in range(2)][1:]
        self._each(chips, lambda slot: self._wait(op, slot, 1 - self.half))


class PlaneShare:
    def __init__(self, traffic, buffer, hand, recv, sems):
        self.traffic, self.buffer, self.hand, self.recv, self.sems, self.number = traffic, buffer, hand, recv, sems, 0
        child, half, row, col = position()
        self.half = half
        self.sibling = (child * 2 + 1 - half, row, col)
        x, y = row // 2, child * 2 + row % 2

        def device(dx, dy):
            place = (y + dy) % 4
            return (place // 2 * 2 + half, (x + dx) % 4 * 2 + place % 2, col)

        def either(first, second):
            return tuple(jnp.where(half == 0, one, two) for one, two in zip(first, second))

        self.first = [either(device(d, 0), device(0, d)) for d in (1, 3)]
        self.second = [either(device(0, d), device(d, 0)) for d in (1, 3)]
        self.slots = []
        for i in range(KR):
            begin_1 = jnp.where(half == 0, i // 2, i % 2)
            begin_2 = jnp.where(half == 0, i % 2, i // 2)
            far_1 = (jnp.where(half == 0, x, y) - begin_1 + 4) % 4
            far_2 = (jnp.where(half == 0, y, x) - begin_2 + 4) % 4
            self.slots.append((i, begin_1, begin_2, far_1, far_2))

    def _send(self, op, i, device):
        block = self.buffer.at[i]
        op.send(block, block, self.sems.at[op.number], self.recv.at[i], device)
        op.number += 1

    def _wait(self, op, i):
        op.landed(self.buffer.at[i], self.recv.at[i])

    def _run(self, cond, body):
        self.number = self.traffic.run(cond, body, self.number)

    def _onward(self, op, i, begin, far, devices):
        pl.when((begin == 1) & (far == 1))(lambda: self._send(op, i, devices[0]))
        pl.when((begin == 0) & (far == 3))(lambda: self._send(op, i, devices[1]))

    def begin(self):
        for i, begin_1, begin_2, far_1, far_2 in self.slots:
            chip = (far_1 == 0) & (far_2 == 0)

            def body(op, i=i):
                @pl.when(self.half == 0)
                def _():
                    hand = self.buffer.at[i] if self.hand is None else self.hand
                    op.send(hand, self.buffer.at[i], self.sems.at[op.number], self.recv.at[i], self.sibling)

                op.number += 1
                pl.when(self.half == 1)(lambda: self._wait(op, i))
                for device in self.first + self.second:
                    self._send(op, i, device)

            self._run(chip, body)

    def relay(self):
        for i, begin_1, begin_2, far_1, far_2 in self.slots:
            def body(op, i=i, begin_1=begin_1, far_1=far_1):
                self._wait(op, i)
                self._onward(op, i, begin_1, far_1, self.first)
                for device in self.second:
                    self._send(op, i, device)

            self._run((far_2 == 0) & (far_1 % 2 == 1), body)

    def relay2(self):
        for i, begin_1, begin_2, far_1, far_2 in self.slots:
            def body(op, i=i):
                self._wait(op, i)
                for device in self.second:
                    self._send(op, i, device)

            self._run((far_2 == 0) & (far_1 == 2), body)

    def relay3(self):
        for i, begin_1, begin_2, far_1, far_2 in self.slots:
            def body(op, i=i, begin_2=begin_2, far_2=far_2):
                self._wait(op, i)
                self._onward(op, i, begin_2, far_2, self.second)

            self._run(far_2 % 2 == 1, body)

    def finish(self):
        op = self.traffic.starter()
        for i, begin_1, begin_2, far_1, far_2 in self.slots:
            pl.when(far_2 == 2)(lambda: self._wait(op, i))


class Line:
    def __init__(self, traffic, buffer, count, recv, sems):
        self.traffic, self.buffer, self.count, self.recv, self.sems = traffic, buffer, count, recv, sems
        child, half, row, col = position()
        self.col = col
        self.places = [(child * 2 + half, row, (col + d) % 8) for d in (1, 7)]

    def _each(self, step, body):
        base = (self.col + step + 8) % 8
        for extra in range((self.count + 7) // 8):
            limit = min(self.count - 8 * extra, 8)

            def run(op, extra=extra, limit=limit):
                body(op, extra, 8 * extra + base % limit)

            self.traffic.run(base < limit, run)

    def begin(self):
        def body(op, extra, slot):
            block = self.buffer.at[slot]
            for way in range(2):
                op.send(block, block, self.sems.at[extra, way], self.recv.at[0, slot], self.places[way])

        self._each(0, body)

    def relay(self, step):
        for way in range(2):
            def body(op, extra, slot, way=way):
                block = self.buffer.at[slot]
                op.landed(block, self.recv.at[0, slot])
                number = 0
                if step == 3:
                    block = self.buffer.at[slot, pl.ds(way * 2 * B, 2 * B)]
                    number = way
                op.send(
                    block, block, self.sems.at[extra, 2 * step + way], self.recv.at[number, slot], self.places[way]
                )

            self._each(step if way else -step, body)

    def finish(self):
        def body(op, extra, slot):
            for way in range(2):
                op.landed(self.buffer.at[slot, pl.ds(way * 2 * B, 2 * B)], self.recv.at[way, slot])

        self._each(4, body)


class TopLine:
    def __init__(self, traffic, count, buffer, recv, sems, owns, mine):
        child, half, row, col = position()
        self.traffic, self.count, self.buffer, self.recv, self.sems = traffic, count, buffer, recv, sems
        self.owns, self.mine, self.col = owns, mine % count, col
        self.depth = count // 2 + 1
        self.places = [(child * 2 + half, row, (col + d) % 8) for d in (1, 7, 2, 6, 3, 5, 4)]

    def held(self):
        for extra in range((self.count + 7) // 8):
            limit = min(self.count - 8 * extra, 8)
            index = 8 * extra + self.col % limit
            place = (index - self.mine + self.count) % self.count
            yield extra, self.owns & (self.col < limit) & (place < self.depth), index, place % self.depth

    def begin(self):
        for extra, cond, index, place in self.held():
            def body(op, extra=extra, index=index, place=place):
                block = self.buffer.at[self.mine, place]
                for n, device in enumerate(self.places):
                    op.send(block, block, self.sems.at[extra, n], self.recv.at[index], device)

            self.traffic.run(cond, body)

    def finish(self):
        op = self.traffic.starter()

        @pl.when(self.owns)
        def _():
            for place in range(self.depth):
                index = (self.mine + place) % self.count

                @pl.when(index % 8 != self.col)
                def _():
                    op.landed(self.buffer.at[self.mine, place], self.recv.at[index])


def greet_all():
    child, half, row, col = position()
    cube = child * 2 + half
    x, y = row // 2, child * 2 + row % 2
    barrier = pltpu.get_barrier_semaphore()
    others = [(cube, row, (col + d) % 8) for d in range(1, 8)]
    others += [(cube, (x + d) % 4 * 2 + row % 2, col) for d in range(1, 4)]
    others += [((y + d) % 4 // 2 * 2 + half, x * 2 + (y + d) % 2, col) for d in range(1, 4)]
    others += [(child * 2 + 1 - half, row, col)]
    for device in others:
        pl.semaphore_signal(barrier, inc=1, device_id=device, device_id_type=MESH)
    return barrier, len(others)


def top_tile(count, top, i, k):
    place = (k - i) % count
    if place <= count // 2:
        return top[i, place].astype(F32)
    return top[k, (i - k) % count].astype(F32).T


def factor_top(count, pair, top, pivots, panels):
    k = 2 * pair
    at = k * B
    first = jnp.concatenate([top_tile(count, top, i, k) for i in range(k, count)], axis=0)
    second = jnp.concatenate([top_tile(count, top, i, k + 1) for i in range(k + 1, count)], axis=0)
    if pair:
        both = dot_nt(panels[at:, :at], panels[at:at + 2 * B, :at])
        first = first - both[:, :B]
        second = second - both[B:, B:]
    first = times_pivot(first, pivots[k]).astype(BF)
    panels[at:, at:at + B] = first
    second = second - dot_nt(first[B:], first[B:2 * B])
    panels[at + B:, at + B:at + 2 * B] = times_pivot(second, pivots[k + 1]).astype(BF)


def factor_own(pair, down, pivots, panels_top, panels, row_class, rows, first_block):
    k = 2 * pair
    at = k * B
    length = rows.stop - rows.start
    block = (lax.broadcasted_iota(jnp.int32, (length, B), 0) + rows.start) // B
    row_block = block == first_block
    first = down[k, rows].astype(F32)
    second = down[k + 1, rows].astype(F32)
    if pair:
        both = dot_nt(panels[rows, :at], panels_top[at:at + 2 * B, :at])
        first = first - both[:, :B]
        second = second - both[:, B:]
    first = times_pivot(first, pivots[k])
    first = jnp.where(row_block & (row_class < k), 0.0, first).astype(BF)
    panels[rows, at:at + B] = first
    second = second - dot_nt(first, panels_top[at + B:at + 2 * B, at:at + B])
    second = times_pivot(second, pivots[k + 1])
    second = jnp.where(row_block & (row_class < k + 1), 0.0, second).astype(BF)
    panels[rows, at + B:at + 2 * B] = second


def factor_wide(pair, side, pivots, panels_top, wide, first_tile):
    k = 2 * pair
    at = k * B
    col_block = lax.broadcasted_iota(jnp.int32, (B, wide.shape[1]), 1) < B
    first = side[k].astype(F32)
    second = side[k + 1].astype(F32)
    if pair:
        both = dot_nn(panels_top[at:at + 2 * B, :at], wide[:at, :])
        first = first - both[:B]
        second = second - both[B:]
    first = pivot_times(pivots[k].T, first)
    first = jnp.where(col_block & (first_tile < k), 0.0, first).astype(BF)
    wide[at:at + B, :] = first
    second = second - dot_nn(panels_top[at + B:at + 2 * B, at:at + B], first)
    second = pivot_times(pivots[k + 1].T, second)
    second = jnp.where(col_block & (first_tile < k + 1), 0.0, second).astype(BF)
    wide[at + B:at + 2 * B, :] = second


def main_kernel(
    fronts, roots, child_pivots, root_pivots,
    panels_out, root_panels_out, rest_out, keep_out, came_out,
    craw, rraw, cwide, rwide, cpiv, rpiv,
    top, down, side, rtop, rdown, rside,
    hand, rhand, ctop, cown, cside, cother, xtop, xown, xside, xother, update,
    load_sem, store_sem, tl_send, tl_recv, rtl_send, rtl_recv, line_send, line_recv, rline_send, rline_recv,
    t_send, t_recv, s_send, s_recv, rt_send, rt_recv, rs_send, rs_recv, u_send, u_recv,
    q_send, q_recv, rq_send, rq_recv,
):
    child, half, row, col = position()
    mine = half * 8 + row
    root_class = child * 16 + mine
    owns = mine < KC
    root_owns = (child == 0) & (half == 0) & (row < KR)

    loads = [
        pltpu.make_async_copy(fronts, craw, load_sem.at[0]),
        pltpu.make_async_copy(child_pivots.at[child], cpiv, load_sem.at[1]),
        pltpu.make_async_copy(roots, rraw, load_sem.at[2]),
        pltpu.make_async_copy(root_pivots, rpiv, load_sem.at[3]),
    ]
    for load in loads:
        load.start()
    barrier, count = greet_all()

    traffic = Traffic()
    top_line = TopLine(traffic, KC, top, tl_recv, tl_send, owns, mine)
    root_top_line = TopLine(traffic, KR, rtop, rtl_recv, rtl_send, root_owns, row)
    line = Line(traffic, down, KC, line_recv, line_send)
    root_line = Line(traffic, rdown, KR, rline_recv, rline_send)
    top_spread = PairSpread(traffic, top, 3, None, t_recv, t_send)
    side_spread = PairSpread(traffic, side, None, hand, s_recv, s_send)
    root_top_spread = PlaneShare(traffic, rtop, None, rt_recv, rt_send)
    root_side_spread = PlaneShare(traffic, rside, rhand, rs_recv, rs_send)
    always = col >= 0

    loads[0].wait()
    for t in range(4):
        cwide[t * 8 * B:(t + 1) * 8 * B, :] = craw[t].astype(F32).reshape(8 * B, B)

    order = [1 - child, 3 - child, child, 2 + child]

    def place_column(line_buffer, count, line_top, wide, stride, order):
        for extra, cond, index, place in line_top.held():
            @pl.when((col + 8 * extra) < count)
            def _():
                for n, t in enumerate(order):
                    column = wide[pl.ds(t * B * stride + extra, B, stride=stride), :]
                    line_buffer[index, n * B:(n + 1) * B] = column.astype(BF)

                @pl.when(cond)
                def _():
                    line_top.buffer[line_top.mine, place] = wide[pl.ds(extra, B, stride=stride), :].astype(BF)

    place_column(down, KC, top_line, cwide, 8, order)
    own_first = 1 + 3 * half
    other_first = 5 - 4 * half

    @pl.when(owns)
    def _():
        for s in range(4):
            columns = slice(s * B, (s + 1) * B)
            side[mine % KC, :, columns] = cwide[pl.ds(own_first + s, B, stride=8), :].astype(BF)
            hand[:, columns] = cwide[pl.ds(4 - 3 * half + s, B, stride=8), :].astype(BF)

    pl.semaphore_wait(barrier, count)
    top_line.begin()
    line.begin()
    side_spread.begin()

    loads[2].wait()
    for t in range(4):
        for b in range(0, B, 32):
            at = (t * B + b) * RS
            rwide[at:at + 32 * RS, :] = rraw[t, b:b + 32].astype(F32).reshape(32 * RS, B)
    place_column(rdown, KR, root_top_line, rwide, RS, range(4))

    @pl.when(root_owns)
    def _():
        for s in range(8):
            columns = slice(s * B, (s + 1) * B)
            rside[row % KR, :, columns] = rwide[pl.ds(s, B, stride=RS), :].astype(BF)
            rhand[:, columns] = rwide[pl.ds(8 + s, B, stride=RS), :].astype(BF)

    root_top_line.begin()
    top_line.finish()
    top_spread.begin()
    line.relay(1)
    top_spread.relay()
    side_spread.relay()
    line.relay(2)
    top_spread.relay2()
    root_top_line.finish()
    root_top_spread.begin()
    root_side_spread.begin()
    side_spread.relay2()
    top_spread.settle()
    line.relay(3)
    root_line.begin()
    top_spread.finish()

    loads[1].wait()
    loads[3].wait()
    for pair in range(2):
        factor_top(KC, pair, top, cpiv, ctop)
    root_top_spread.relay()
    root_side_spread.relay()
    for pair in range(2, 4):
        factor_top(KC, pair, top, cpiv, ctop)
    root_top_spread.relay2()
    root_side_spread.relay2()
    root_line.relay(1)
    factor_top(KC, 4, top, cpiv, ctop)
    line.finish()
    side_spread.settle()

    sibling = (child * 2 + 1 - half, row, col)
    partner = ((1 - child) * 2 + half, row, col)
    first_block = jnp.where(child == 1, 0, 2)

    def to_sibling(buffer, other, pair, send_sem, recv_sem):
        block = pl.ds(2 * pair * B, 2 * B)

        def body(op):
            op.send(buffer.at[block], other.at[block], send_sem.at[pair], recv_sem.at[pair], sibling)

        traffic.run(always, body)

    def from_sibling(other, pair, recv_sem):
        Starter().landed(other.at[pl.ds(2 * pair * B, 2 * B)], recv_sem.at[pair])

    def update_own(n):
        product = dot_nn(cown[n * B:(n + 1) * B, :], cside[...])
        for s in range(4):
            value = cwide[pl.ds(order[n] * 8 * B + own_first + s, B, stride=8), :]
            update[n, :, s * B:(s + 1) * B] = (value - product[:, s * B:(s + 1) * B]).astype(BF)

    def update_other(n):
        columns = pl.ds(pl.multiple_of((1 - half) * B, B), 3 * B)
        product = dot_nn(cown[n * B:(n + 1) * B, :], cother[:, columns])
        for s in range(3):
            value = cwide[pl.ds(order[n] * 8 * B + other_first + s, B, stride=8), :]
            update[n, :, (4 + s) * B:(5 + s) * B] = (value - product[:, s * B:(s + 1) * B]).astype(BF)

    def send_update(n, part):
        columns = pl.ds(0, 4 * B) if part == 0 else pl.ds(4 * B, 3 * B)

        def body(op):
            op.send(
                update.at[n, :, columns], came_out.at[n, :, columns],
                u_send.at[part, n], u_recv.at[part, n], partner,
            )

        traffic.run(always, body)

    for pair in range(KC // 2):
        factor_wide(pair, side, cpiv, ctop, cside, 8 + 24 * half + col)
        factor_own(pair, down, cpiv, ctop, cown, mine, slice(0, 2 * B), first_block)
        to_sibling(cside, cother, pair, q_send, q_recv)
    root_top_spread.relay3()
    root_side_spread.relay3()
    for n in range(2):
        update_own(n)
        send_update(n, 0)
    for pair in range(KC // 2):
        from_sibling(cother, pair, q_recv)
    for n in range(2):
        update_other(n)
        send_update(n, 1)
    root_line.relay(2)
    for pair in range(KC // 2):
        factor_own(pair, down, cpiv, ctop, cown, mine, slice(2 * B, 4 * B), first_block)
    panels_stores = []
    for n in range(4):
        rows = pl.ds(pl.multiple_of(order[n] * B, B), B)
        panels_stores.append(
            pltpu.make_async_copy(cown.at[pl.ds(n * B, B)], panels_out.at[rows], store_sem.at[8 + n])
        )
        panels_stores[-1].start()
    for n in range(2, 4):
        update_own(n)
        update_other(n)
    keep_store = pltpu.make_async_copy(update.at[pl.ds(2, 2)], keep_out, store_sem.at[0])
    keep_store.start()
    root_line.relay(3)

    root_top_spread.finish()
    for pair in range(KR // 2):
        factor_top(KR, pair, rtop, rpiv, xtop)
    root_side_spread.finish()
    for pair in range(KR // 2):
        factor_wide(pair, rside, rpiv, xtop, xside, 64 * half + col)
        to_sibling(xside, xother, pair, rq_send, rq_recv)
    root_line.finish()
    for pair in range(KR // 2):
        factor_own(pair, rdown, rpiv, xtop, xown, root_class, slice(0, 4 * B), 0)
    root_panels_store = pltpu.make_async_copy(xown, root_panels_out, store_sem.at[3])
    root_panels_store.start()
    for pair in range(KR // 2):
        from_sibling(xother, pair, rq_recv)
    rest_stores = []
    for t in range(4):
        for buffer, first in ((xside, 8 * half), (xother, 8 - 8 * half)):
            product = dot_nn(xown[t * B:(t + 1) * B, :], buffer[...])
            for s in range(8):
                place = pl.ds(t * RS * B + first + s, B, stride=RS)
                rwide[place, :] = rwide[place, :] - product[:, s * B:(s + 1) * B]
        block = pl.ds(t * RS * B, RS * B)
        rest_stores.append(pltpu.make_async_copy(rwide.at[block], rest_out.at[block], store_sem.at[4 + t]))
        rest_stores[-1].start()

    for n in range(2):
        Starter().landed(came_out.at[n, :, pl.ds(0, 4 * B)], u_recv.at[0, n])
        Starter().landed(came_out.at[n, :, pl.ds(4 * B, 3 * B)], u_recv.at[1, n])
    traffic.drain()
    for store in [keep_store, root_panels_store] + panels_stores + rest_stores:
        store.wait()


def main_step(fronts, roots, child_pivots, root_pivots):
    dma = pltpu.SemaphoreType.DMA
    anywhere = pl.BlockSpec(memory_space=pltpu.HBM)
    return pl.pallas_call(
        main_kernel,
        out_shape=[
            jax.ShapeDtypeStruct((4 * B, KC * B), BF),
            jax.ShapeDtypeStruct((4 * B, KR * B), BF),
            jax.ShapeDtypeStruct((4 * B * RS, B), F32),
            jax.ShapeDtypeStruct((2, B, CS * B), BF),
            jax.ShapeDtypeStruct((2, B, CS * B), BF),
        ],
        in_specs=[anywhere] * 4,
        out_specs=[anywhere] * 5,
        scratch_shapes=[
            pltpu.VMEM((4, B, 8, B), BF),
            pltpu.VMEM((4, B, RS, B), BF),
            pltpu.VMEM((4 * B * 8, B), F32),
            pltpu.VMEM((4 * B * RS, B), F32),
            pltpu.VMEM((KC, B, B), F32),
            pltpu.VMEM((KR, B, B), F32),
            pltpu.VMEM((KC, KC // 2 + 1, B, B), BF),
            pltpu.VMEM((KC, 4 * B, B), BF),
            pltpu.VMEM((KC, B, 4 * B), BF),
            pltpu.VMEM((KR, KR // 2 + 1, B, B), BF),
            pltpu.VMEM((KR, 4 * B, B), BF),
            pltpu.VMEM((KR, B, 8 * B), BF),
            pltpu.VMEM((B, 4 * B), BF),
            pltpu.VMEM((B, 8 * B), BF),
            pltpu.VMEM((KC * B, KC * B), BF),
            pltpu.VMEM((4 * B, KC * B), BF),
            pltpu.VMEM((KC * B, 4 * B), BF),
            pltpu.VMEM((KC * B, 4 * B), BF),
            pltpu.VMEM((KR * B, KR * B), BF),
            pltpu.VMEM((4 * B, KR * B), BF),
            pltpu.VMEM((KR * B, 8 * B), BF),
            pltpu.VMEM((KR * B, 8 * B), BF),
            pltpu.VMEM((4, B, CS * B), BF),
            dma((4,)), dma((12,)),
            dma((2, 7)), dma((KC,)), dma((1, 7)), dma((KR,)),
            dma((2, 8)), dma((2, KC)), dma((1, 8)), dma((2, KR)),
            dma((64,)), dma((2, KC)), dma((64,)), dma((1, KC)),
            dma((64,)), dma((KR,)), dma((64,)), dma((KR,)),
            dma((2, 2)), dma((2, 2)), dma((5,)), dma((5,)), dma((2,)), dma((2,)),
        ],
        compiler_params=pltpu.CompilerParams(
            collective_id=0, has_side_effects=True, vmem_limit_bytes=56 * 2**20
        ),
        cost_estimate=pl.CostEstimate(flops=10**10, bytes_accessed=10**7, transcendentals=0),
    )(fronts, roots, child_pivots, root_pivots)


def add_kernel(maps, rest, keep, came, panels, root_panels, out, panels_out, root_panels_out, total, tiles, done, sems):
    child, half, row, col = position()
    passes = [
        pltpu.make_async_copy(panels, panels_out, sems.at[0]),
        pltpu.make_async_copy(root_panels, root_panels_out, sems.at[1]),
    ]
    fetch = [pltpu.make_async_copy(source, tiles.at[n], sems.at[2 + n]) for n, source in enumerate((keep, came))]
    height = RS * B
    blocks = [pl.ds(t * height, height) for t in range(4)]
    fetch += [pltpu.make_async_copy(rest.at[blocks[t]], total.at[blocks[t]], sems.at[4 + t]) for t in range(4)]
    for copy in fetch + passes:
        copy.start()
    for copy in fetch:
        copy.wait()
    for number, source in enumerate((child, 1 - child)):
        for p in range(2):
            i = (2 * p + child) * 16 + half * 8 + row - KC
            for n in range(7):
                s = 1 + 3 * half + n if n < 4 else 1 - 4 * half + n
                j = s * 8 + col - KC

                @pl.when((i >= 0) & (j >= 0))
                def _():
                    below = maps[source, jnp.maximum(i, 0)] // 32
                    across = maps[source, jnp.maximum(j, 0)] // 8
                    place = pl.ds(below * height + across, B, stride=RS)
                    total[place, :] = total[place, :] + tiles[number, p, :, n * B:(n + 1) * B].astype(F32)
    stores = []
    for t in range(4):
        for b in range(0, B, 32):
            at = (t * B + b) * RS
            done[t, b:b + 32] = total[at:at + 32 * RS, :].astype(BF).reshape(32, RS, B)
        stores.append(pltpu.make_async_copy(done.at[t], out.at[t], sems.at[8 + t]))
        stores[-1].start()
    for copy in stores + passes:
        copy.wait()


def add_step(maps, rest, keep, came, panels, root_panels):
    anywhere = pl.BlockSpec(memory_space=pltpu.HBM)
    return pl.pallas_call(
        add_kernel,
        out_shape=[
            jax.ShapeDtypeStruct((4, B, RS, B), BF),
            jax.ShapeDtypeStruct((4 * B, KC * B), BF),
            jax.ShapeDtypeStruct((4 * B, KR * B), BF),
        ],
        in_specs=[pl.BlockSpec(memory_space=pltpu.SMEM)] + [anywhere] * 5,
        out_specs=[anywhere] * 3,
        scratch_shapes=[
            pltpu.VMEM((4 * B * RS, B), F32),
            pltpu.VMEM((2, 2, B, CS * B), BF),
            pltpu.VMEM((4, B, RS, B), BF),
            pltpu.SemaphoreType.DMA((12,)),
        ],
        compiler_params=pltpu.CompilerParams(vmem_limit_bytes=48 * 2**20),
    )(maps, rest, keep, came, panels, root_panels)


def on_device(child_fronts, root_front, child_pivots, root_pivots, child_maps):
    fronts = child_fronts.reshape(4, B, 8, B)
    roots = root_front.reshape(4, B, RS, B)
    panels, root_panels, rest, keep, came = main_step(fronts, roots, child_pivots, root_pivots)
    root_rest, panels, root_panels = add_step(child_maps, rest, keep, came, panels, root_panels)
    return (
        panels.reshape(4, 1, B, KC * B),
        root_panels.reshape(4, 1, B, KR * B),
        root_rest.reshape(4, 1, B, RS, 1, B),
    )


def solution(mesh):
    placed = (
        P(None, ("cube", "row"), None, None, "col", None),
        P(None, ("cube", "row"), None, None, "col", None),
        P(),
        P(),
        P(),
    )
    return jax.shard_map(
        on_device,
        mesh=mesh,
        in_specs=placed,
        out_specs=(
            P(None, ("cube", "row"), None, None),
            P(None, ("cube", "row"), None, None),
            P(None, ("cube", "row"), None, None, "col", None),
        ),
        check_vma=False,
    )
```

```python
import functools

import jax
import jax.numpy as jnp
from jax import lax
from jax.experimental import pallas as pl
from jax.experimental.pallas import tpu as pltpu
from jax.sharding import PartitionSpec as P

B = 128
KC = 10
KR = 4
CS = 7
RS = 16
MESH = pl.DeviceIdType.MESH
BF = jnp.bfloat16
F32 = jnp.float32


def dot_nn(left, right):
    return lax.dot_general(left, right, (((1,), (0,)), ((), ())), preferred_element_type=F32)


def dot_nt(left, right):
    return lax.dot_general(left, right, (((1,), (1,)), ((), ())), preferred_element_type=F32)


def split(value):
    high = value.astype(BF)
    return high, (value - high.astype(F32)).astype(BF)


def times_pivot(value, pivot):
    pivot_high, pivot_low = split(pivot)
    upper = jnp.concatenate([pivot_high, pivot_low], axis=1)
    lower = jnp.concatenate([pivot_high, jnp.zeros_like(pivot_low)], axis=1)
    product = dot_nn(jnp.concatenate(split(value), axis=1), jnp.concatenate([upper, lower], axis=0))
    return product[:, :B] + product[:, B:]


def pivot_times(pivot_t, value):
    pivot_high, pivot_low = split(pivot_t)
    upper = jnp.concatenate([pivot_high, pivot_high], axis=1)
    lower = jnp.concatenate([pivot_low, jnp.zeros_like(pivot_low)], axis=1)
    product = dot_nn(jnp.concatenate([upper, lower], axis=0), jnp.concatenate(split(value), axis=0))
    return product[:B] + product[B:]


def position():
    cube = lax.axis_index("cube")
    return cube // 2, cube % 2, lax.axis_index("row"), lax.axis_index("col")


class Starter:
    def __init__(self, number=0):
        self.number = number

    def send(self, source, target, send_sem, recv_sem, device):
        remote(source, target, send_sem, recv_sem, device).start()

    def landed(self, block, recv_sem):
        child, half, row, col = position()
        remote(block, block, recv_sem, recv_sem, (child * 2 + 1 - half, row, col)).wait_recv()


class Drainer:
    def __init__(self, number=0):
        self.number = number

    def send(self, source, target, send_sem, recv_sem, device):
        remote(source, target, send_sem, recv_sem, device).wait_send()

    def landed(self, block, recv_sem):
        pass


def remote(source, target, send_sem, recv_sem, device):
    return pltpu.make_async_remote_copy(
        src_ref=source, dst_ref=target, send_sem=send_sem, recv_sem=recv_sem,
        device_id=device, device_id_type=MESH,
    )


class Traffic:
    def __init__(self):
        self.pending = []

    def starter(self):
        return Starter()

    def run(self, cond, body, number=0):
        op = Starter(number)
        pl.when(cond)(lambda: body(op))
        self.pending.append((cond, body, number))
        return op.number

    def drain(self):
        for cond, body, number in self.pending:
            pl.when(cond)(lambda: body(Drainer(number)))
        self.pending = []


class PairSpread:
    def __init__(self, traffic, buffer, size, hand, recv, sems):
        self.traffic, self.buffer, self.size, self.hand = traffic, buffer, size, hand
        self.recv, self.sems, self.number = recv, sems, 0
        child, half, row, col = position()
        self.half, self.row, self.x, self.y = half, row, row // 2, row % 2
        self.sibling = (child * 2 + 1 - half, row, col)
        self.plus, self.minus = [(child * 2 + half, (self.x + d) % 4 * 2 + self.y, col) for d in (1, 3)]
        self.across = (child * 2 + half, row + 1 - 2 * self.y, col)
        self.mine = half * 8 + row
        self.other = (1 - half) * 8 + row

    def part(self, slot, half):
        if self.size is None:
            return self.buffer.at[slot], self.recv.at[0, slot]
        start = pl.multiple_of(half * self.size, self.size)
        return self.buffer.at[slot, pl.ds(start, self.size)], self.recv.at[half, slot]

    def _send(self, op, slot, device, half=None):
        block, recv = self.part(slot, self.half if half is None else half)
        op.send(block, block, self.sems.at[op.number], recv, device)
        op.number += 1

    def _wait(self, op, slot, half=None):
        block, recv = self.part(slot, self.half if half is None else half)
        op.landed(block, recv)

    def _pass(self, op, slot):
        if self.size is not None:
            self._send(op, slot, self.sibling)

    def _run(self, cond, body):
        self.number = self.traffic.run(cond, body, self.number)

    def _each(self, chips, body):
        for chip in chips:
            body(chip)
            pl.when(chip < 2)(lambda: body(8 + chip % 2))

    def _row(self, d, e):
        return (self.x + d) % 4 * 2 + (self.y + e) % 2

    def begin(self):
        def own(op):
            slot = self.mine % KC
            if self.size is None:
                block, recv = self.part(slot, self.half)
                op.send(self.hand, block, self.sems.at[op.number], recv, self.sibling)
                op.number += 1
            else:
                self._send(op, slot, self.sibling, 1 - self.half)
            for device in (self.across, self.plus, self.minus):
                self._send(op, slot, device)
            self._pass(op, slot)

        def others(op):
            slot = self.other % KC
            self._wait(op, slot)
            for device in (self.across, self.plus, self.minus):
                self._send(op, slot, device)

        self._run(self.mine < KC, own)
        self._run(self.other < KC, others)

    def _onward(self, op, slot, d):
        if d == 3:
            pl.when(slot < 4)(lambda: self._send(op, slot, self.plus))
        else:
            pl.when(slot >= 4)(lambda: self._send(op, slot, self.minus))

    def relay(self):
        def first(op):
            for d in (3, 1):
                def body(slot):
                    self._wait(op, slot)
                    self._onward(op, slot, d)
                    self._send(op, slot, self.across)
                    self._pass(op, slot)

                self._each([self._row(d, 0)], body)

        def second(op):
            def body(slot):
                self._wait(op, slot)
                self._send(op, slot, self.plus)
                self._send(op, slot, self.minus)
                self._pass(op, slot)

            self._each([self._row(0, 1)], body)

        self._run(self.half == 0, first)
        self._run(self.half == 1, second)

    def relay2(self):
        def first(op):
            def body(slot):
                self._wait(op, slot)
                self._send(op, slot, self.across)
                self._pass(op, slot)

            self._each([self._row(2, 0)], body)

        def second(op):
            for e in range(2):
                for d in (3, 1):
                    def body(slot):
                        self._wait(op, slot)
                        self._onward(op, slot, d)
                        self._pass(op, slot)

                    self._each([self._row(d, e)], body)

        self._run(self.half == 0, first)
        self._run(self.half == 1, second)

    def settle(self):
        def body(op, slot):
            self._wait(op, slot)
            self._pass(op, slot)

        def first(op):
            self._each([self._row(d, 1) for d in (0, 3, 1, 2)], lambda slot: body(op, slot))

        def second(op):
            self._each([self._row(2, e) for e in range(2)], lambda slot: body(op, slot))

        self._run(self.half == 0, first)
        self._run(self.half == 1, second)

    def finish(self):
        if self.size is None:
            return
        op = self.traffic.starter()
        pl.when(self.other < KC)(lambda: self._wait(op, self.other % KC, 1 - self.half))
        chips = [self._row(d, e) for d in range(4) for e in range(2)][1:]
        self._each(chips, lambda slot: self._wait(op, slot, 1 - self.half))


class PlaneShare:
    def __init__(self, traffic, buffer, hand, recv, sems):
        self.traffic, self.buffer, self.hand, self.recv, self.sems, self.number = traffic, buffer, hand, recv, sems, 0
        child, half, row, col = position()
        self.half = half
        self.sibling = (child * 2 + 1 - half, row, col)
        x, y = row // 2, child * 2 + row % 2

        def device(dx, dy):
            place = (y + dy) % 4
            return (place // 2 * 2 + half, (x + dx) % 4 * 2 + place % 2, col)

        def either(first, second):
            return tuple(jnp.where(half == 0, one, two) for one, two in zip(first, second))

        self.first = [either(device(d, 0), device(0, d)) for d in (1, 3)]
        self.second = [either(device(0, d), device(d, 0)) for d in (1, 3)]
        self.slots = []
        for i in range(KR):
            begin_1 = jnp.where(half == 0, i // 2, i % 2)
            begin_2 = jnp.where(half == 0, i % 2, i // 2)
            far_1 = (jnp.where(half == 0, x, y) - begin_1 + 4) % 4
            far_2 = (jnp.where(half == 0, y, x) - begin_2 + 4) % 4
            self.slots.append((i, begin_1, begin_2, far_1, far_2))

    def _send(self, op, i, device):
        block = self.buffer.at[i]
        op.send(block, block, self.sems.at[op.number], self.recv.at[i], device)
        op.number += 1

    def _wait(self, op, i):
        op.landed(self.buffer.at[i], self.recv.at[i])

    def _run(self, cond, body):
        self.number = self.traffic.run(cond, body, self.number)

    def _onward(self, op, i, begin, far, devices):
        pl.when((begin == 1) & (far == 1))(lambda: self._send(op, i, devices[0]))
        pl.when((begin == 0) & (far == 3))(lambda: self._send(op, i, devices[1]))

    def begin(self):
        for i, begin_1, begin_2, far_1, far_2 in self.slots:
            chip = (far_1 == 0) & (far_2 == 0)

            def body(op, i=i):
                @pl.when(self.half == 0)
                def _():
                    hand = self.buffer.at[i] if self.hand is None else self.hand
                    op.send(hand, self.buffer.at[i], self.sems.at[op.number], self.recv.at[i], self.sibling)

                op.number += 1
                pl.when(self.half == 1)(lambda: self._wait(op, i))
                for device in self.first + self.second:
                    self._send(op, i, device)

            self._run(chip, body)

    def relay(self):
        for i, begin_1, begin_2, far_1, far_2 in self.slots:
            def body(op, i=i, begin_1=begin_1, far_1=far_1):
                self._wait(op, i)
                self._onward(op, i, begin_1, far_1, self.first)
                for device in self.second:
                    self._send(op, i, device)

            self._run((far_2 == 0) & (far_1 % 2 == 1), body)

    def relay2(self):
        for i, begin_1, begin_2, far_1, far_2 in self.slots:
            def body(op, i=i):
                self._wait(op, i)
                for device in self.second:
                    self._send(op, i, device)

            self._run((far_2 == 0) & (far_1 == 2), body)

    def relay3(self):
        for i, begin_1, begin_2, far_1, far_2 in self.slots:
            def body(op, i=i, begin_2=begin_2, far_2=far_2):
                self._wait(op, i)
                self._onward(op, i, begin_2, far_2, self.second)

            self._run(far_2 % 2 == 1, body)

    def finish(self):
        op = self.traffic.starter()
        for i, begin_1, begin_2, far_1, far_2 in self.slots:
            pl.when(far_2 == 2)(lambda: self._wait(op, i))


class Line:
    def __init__(self, traffic, buffer, count, recv, sems):
        self.traffic, self.buffer, self.count, self.recv, self.sems = traffic, buffer, count, recv, sems
        child, half, row, col = position()
        self.col = col
        self.places = [(child * 2 + half, row, (col + d) % 8) for d in (1, 7)]

    def _each(self, step, body):
        base = (self.col + step + 8) % 8
        for extra in range((self.count + 7) // 8):
            limit = min(self.count - 8 * extra, 8)

            def run(op, extra=extra, limit=limit):
                body(op, extra, 8 * extra + base % limit)

            self.traffic.run(base < limit, run)

    def begin(self):
        def body(op, extra, slot):
            block = self.buffer.at[slot]
            for way in range(2):
                op.send(block, block, self.sems.at[extra, way], self.recv.at[0, slot], self.places[way])

        self._each(0, body)

    def relay(self, step):
        for way in range(2):
            def body(op, extra, slot, way=way):
                block = self.buffer.at[slot]
                op.landed(block, self.recv.at[0, slot])
                number = 0
                if step == 3:
                    block = self.buffer.at[slot, pl.ds(way * 2 * B, 2 * B)]
                    number = way
                op.send(
                    block, block, self.sems.at[extra, 2 * step + way], self.recv.at[number, slot], self.places[way]
                )

            self._each(step if way else -step, body)

    def finish(self):
        def body(op, extra, slot):
            for way in range(2):
                op.landed(self.buffer.at[slot, pl.ds(way * 2 * B, 2 * B)], self.recv.at[way, slot])

        self._each(4, body)


class TopLine:
    def __init__(self, traffic, count, buffer, recv, sems, owns, mine):
        child, half, row, col = position()
        self.traffic, self.count, self.buffer, self.recv, self.sems = traffic, count, buffer, recv, sems
        self.owns, self.mine, self.col = owns, mine % count, col
        self.depth = count // 2 + 1
        self.places = [(child * 2 + half, row, (col + d) % 8) for d in (1, 7, 2, 6, 3, 5, 4)]

    def held(self):
        for extra in range((self.count + 7) // 8):
            limit = min(self.count - 8 * extra, 8)
            index = 8 * extra + self.col % limit
            place = (index - self.mine + self.count) % self.count
            yield extra, self.owns & (self.col < limit) & (place < self.depth), index, place % self.depth

    def begin(self):
        for extra, cond, index, place in self.held():
            def body(op, extra=extra, index=index, place=place):
                block = self.buffer.at[self.mine, place]
                for n, device in enumerate(self.places):
                    op.send(block, block, self.sems.at[extra, n], self.recv.at[index], device)

            self.traffic.run(cond, body)

    def finish(self):
        op = self.traffic.starter()

        @pl.when(self.owns)
        def _():
            for place in range(self.depth):
                index = (self.mine + place) % self.count

                @pl.when(index % 8 != self.col)
                def _():
                    op.landed(self.buffer.at[self.mine, place], self.recv.at[index])


def greet_all():
    child, half, row, col = position()
    cube = child * 2 + half
    x, y = row // 2, child * 2 + row % 2
    barrier = pltpu.get_barrier_semaphore()
    others = [(cube, row, (col + d) % 8) for d in range(1, 8)]
    others += [(cube, (x + d) % 4 * 2 + row % 2, col) for d in range(1, 4)]
    others += [((y + d) % 4 // 2 * 2 + half, x * 2 + (y + d) % 2, col) for d in range(1, 4)]
    others += [(child * 2 + 1 - half, row, col)]
    for device in others:
        pl.semaphore_signal(barrier, inc=1, device_id=device, device_id_type=MESH)
    return barrier, len(others)


def top_tile(count, top, i, k):
    place = (k - i) % count
    if place <= count // 2:
        return top[i, place].astype(F32)
    return top[k, (i - k) % count].astype(F32).T


def factor_top(count, pair, top, pivots, panels):
    k = 2 * pair
    at = k * B
    first = jnp.concatenate([top_tile(count, top, i, k) for i in range(k, count)], axis=0)
    second = jnp.concatenate([top_tile(count, top, i, k + 1) for i in range(k + 1, count)], axis=0)
    if pair:
        both = dot_nt(panels[at:, :at], panels[at:at + 2 * B, :at])
        first = first - both[:, :B]
        second = second - both[B:, B:]
    first = times_pivot(first, pivots[k]).astype(BF)
    panels[at:, at:at + B] = first
    second = second - dot_nt(first[B:], first[B:2 * B])
    panels[at + B:, at + B:at + 2 * B] = times_pivot(second, pivots[k + 1]).astype(BF)


def factor_own(pair, down, pivots, panels_top, panels, row_class, rows, first_block):
    k = 2 * pair
    at = k * B
    length = rows.stop - rows.start
    block = (lax.broadcasted_iota(jnp.int32, (length, B), 0) + rows.start) // B
    row_block = block == first_block
    first = down[k, rows].astype(F32)
    second = down[k + 1, rows].astype(F32)
    if pair:
        both = dot_nt(panels[rows, :at], panels_top[at:at + 2 * B, :at])
        first = first - both[:, :B]
        second = second - both[:, B:]
    first = times_pivot(first, pivots[k])
    first = jnp.where(row_block & (row_class < k), 0.0, first).astype(BF)
    panels[rows, at:at + B] = first
    second = second - dot_nt(first, panels_top[at + B:at + 2 * B, at:at + B])
    second = times_pivot(second, pivots[k + 1])
    second = jnp.where(row_block & (row_class < k + 1), 0.0, second).astype(BF)
    panels[rows, at + B:at + 2 * B] = second


def factor_wide(pair, side, pivots, panels_top, wide, first_tile):
    k = 2 * pair
    at = k * B
    col_block = lax.broadcasted_iota(jnp.int32, (B, wide.shape[1]), 1) < B
    first = side[k].astype(F32)
    second = side[k + 1].astype(F32)
    if pair:
        both = dot_nn(panels_top[at:at + 2 * B, :at], wide[:at, :])
        first = first - both[:B]
        second = second - both[B:]
    first = pivot_times(pivots[k].T, first)
    first = jnp.where(col_block & (first_tile < k), 0.0, first).astype(BF)
    wide[at:at + B, :] = first
    second = second - dot_nn(panels_top[at + B:at + 2 * B, at:at + B], first)
    second = pivot_times(pivots[k + 1].T, second)
    second = jnp.where(col_block & (first_tile < k + 1), 0.0, second).astype(BF)
    wide[at + B:at + 2 * B, :] = second


def main_kernel(
    fronts, roots, child_pivots, root_pivots,
    panels_out, xown, rest, keep_out, came_out,
    craw, rraw, cwide, rwide, ctile, rtile, cpiv, rpiv,
    top, down, side, rtop, rdown, rside,
    hand, rhand, ctop, cown, cside, cother, xtop, xside, xother, update,
    load_sem, store_sem, tl_send, tl_recv, rtl_send, rtl_recv, line_send, line_recv, rline_send, rline_recv,
    t_send, t_recv, s_send, s_recv, rt_send, rt_recv, rs_send, rs_recv, u_send, u_recv,
    q_send, q_recv, rq_send, rq_recv,
):
    child, half, row, col = position()
    mine = half * 8 + row
    root_class = child * 16 + mine
    owns = mine < KC
    root_owns = (child == 0) & (half == 0) & (row < KR)

    loads = [
        pltpu.make_async_copy(fronts, craw, load_sem.at[0]),
        pltpu.make_async_copy(child_pivots.at[child], cpiv, load_sem.at[1]),
        pltpu.make_async_copy(roots, rraw, load_sem.at[2]),
        pltpu.make_async_copy(root_pivots, rpiv, load_sem.at[3]),
    ]
    for load in loads:
        load.start()
    barrier, count = greet_all()

    traffic = Traffic()
    top_line = TopLine(traffic, KC, top, tl_recv, tl_send, owns, mine)
    root_top_line = TopLine(traffic, KR, rtop, rtl_recv, rtl_send, root_owns, row)
    line = Line(traffic, down, KC, line_recv, line_send)
    root_line = Line(traffic, rdown, KR, rline_recv, rline_send)
    top_spread = PairSpread(traffic, top, 3, None, t_recv, t_send)
    side_spread = PairSpread(traffic, side, None, hand, s_recv, s_send)
    root_top_spread = PlaneShare(traffic, rtop, None, rt_recv, rt_send)
    root_side_spread = PlaneShare(traffic, rside, rhand, rs_recv, rs_send)
    always = col >= 0

    order = [1 - child, 3 - child, child, 2 + child]
    own_first = 1 + 3 * half
    other_first = 5 - 4 * half

    def part_tiles(raw, wide, tiles, t):
        stride = raw.shape[2]
        for b in range(0, B, 32):
            at = b * stride
            wide[at:at + 32 * stride, :] = raw[t, b:b + 32].astype(F32).reshape(32 * stride, B)
        for s in range(stride):
            tiles[s, t] = wide[pl.ds(s, B, stride=stride), :].astype(BF)

    def place_top(line_top, tiles):
        for extra, cond, index, place in line_top.held():
            @pl.when(cond)
            def _():
                line_top.buffer[line_top.mine, place] = tiles[extra, 0]

    def place_columns(line_buffer, count, line_top, tiles, order):
        for extra, cond, index, place in line_top.held():
            @pl.when((col + 8 * extra) < count)
            def _():
                for n, t in enumerate(order):
                    line_buffer[index, n * B:(n + 1) * B] = tiles[extra, t]

    loads[0].wait()
    part_tiles(craw, cwide.at[0], ctile, 0)
    place_top(top_line, ctile)
    pl.semaphore_wait(barrier, count)
    top_line.begin()
    for t in range(1, 4):
        part_tiles(craw, cwide.at[t], ctile, t)
    place_columns(down, KC, top_line, ctile, order)
    line.begin()

    @pl.when(owns)
    def _():
        for s in range(4):
            columns = slice(s * B, (s + 1) * B)
            side[mine % KC, :, columns] = ctile[own_first + s, 0]
            hand[:, columns] = ctile[4 - 3 * half + s, 0]

    loads[2].wait()
    for t in range(4):
        part_tiles(rraw, rwide.at[t], rtile, t)
    place_top(root_top_line, rtile)
    place_columns(rdown, KR, root_top_line, rtile, range(4))

    @pl.when(root_owns)
    def _():
        for s in range(8):
            columns = slice(s * B, (s + 1) * B)
            rside[row % KR, :, columns] = rtile[s, 0]
            rhand[:, columns] = rtile[8 + s, 0]

    root_top_line.begin()
    top_line.finish()
    top_spread.begin()
    side_spread.begin()
    line.relay(1)
    top_spread.relay()
    side_spread.relay()
    line.relay(2)
    top_spread.relay2()
    root_top_line.finish()
    root_top_spread.begin()
    root_side_spread.begin()
    side_spread.relay2()
    top_spread.settle()
    line.relay(3)
    root_line.begin()
    top_spread.finish()

    loads[1].wait()
    loads[3].wait()
    for pair in range(2):
        factor_top(KC, pair, top, cpiv, ctop)
    root_top_spread.relay()
    root_side_spread.relay()
    for pair in range(2, 4):
        factor_top(KC, pair, top, cpiv, ctop)
    root_top_spread.relay2()
    root_side_spread.relay2()
    root_line.relay(1)
    factor_top(KC, 4, top, cpiv, ctop)
    line.finish()
    side_spread.settle()

    sibling = (child * 2 + 1 - half, row, col)
    partner = ((1 - child) * 2 + half, row, col)
    first_block = jnp.where(child == 1, 0, 2)

    def to_sibling(buffer, other, pair, send_sem, recv_sem):
        block = pl.ds(2 * pair * B, 2 * B)

        def body(op):
            op.send(buffer.at[block], other.at[block], send_sem.at[pair], recv_sem.at[pair], sibling)

        traffic.run(always, body)

    def from_sibling(other, pair, recv_sem):
        Starter().landed(other.at[pl.ds(2 * pair * B, 2 * B)], recv_sem.at[pair])

    def update_own(n):
        product = dot_nn(cown[n * B:(n + 1) * B, :], cside[...])
        for s in range(4):
            value = ctile[own_first + s, order[n]].astype(F32)
            update[n, :, s * B:(s + 1) * B] = (value - product[:, s * B:(s + 1) * B]).astype(BF)

    def update_other(n):
        columns = pl.ds(pl.multiple_of((1 - half) * B, B), 3 * B)
        product = dot_nn(cown[n * B:(n + 1) * B, :], cother[:, columns])
        for s in range(3):
            value = ctile[other_first + s, order[n]].astype(F32)
            update[n, :, (4 + s) * B:(5 + s) * B] = (value - product[:, s * B:(s + 1) * B]).astype(BF)

    def send_update(n, part):
        columns = pl.ds(0, 4 * B) if part == 0 else pl.ds(4 * B, 3 * B)

        def body(op):
            op.send(
                update.at[n, :, columns], came_out.at[n, :, columns],
                u_send.at[part, n], u_recv.at[part, n], partner,
            )

        traffic.run(always, body)

    for pair in range(KC // 2):
        factor_wide(pair, side, cpiv, ctop, cside, 8 + 24 * half + col)
        factor_own(pair, down, cpiv, ctop, cown, mine, slice(0, 2 * B), first_block)
        to_sibling(cside, cother, pair, q_send, q_recv)
    root_top_spread.relay3()
    root_side_spread.relay3()
    for n in range(2):
        update_own(n)
        send_update(n, 0)
    for pair in range(KC // 2):
        from_sibling(cother, pair, q_recv)
    for n in range(2):
        update_other(n)
        send_update(n, 1)
    root_line.relay(2)
    for pair in range(KC // 2):
        factor_own(pair, down, cpiv, ctop, cown, mine, slice(2 * B, 4 * B), first_block)
    panels_stores = []
    for n in range(4):
        rows = pl.ds(pl.multiple_of(order[n] * B, B), B)
        panels_stores.append(
            pltpu.make_async_copy(cown.at[pl.ds(n * B, B)], panels_out.at[rows], store_sem.at[8 + n])
        )
        panels_stores[-1].start()
    for n in range(2, 4):
        update_own(n)
        update_other(n)
    keep_store = pltpu.make_async_copy(update.at[pl.ds(2, 2)], keep_out, store_sem.at[0])
    keep_store.start()
    root_line.relay(3)

    root_top_spread.finish()
    for pair in range(KR // 2):
        factor_top(KR, pair, rtop, rpiv, xtop)
    root_side_spread.finish()
    for pair in range(KR // 2):
        factor_wide(pair, rside, rpiv, xtop, xside, 64 * half + col)
        to_sibling(xside, xother, pair, rq_send, rq_recv)
    root_line.finish()
    for pair in range(KR // 2):
        factor_own(pair, rdown, rpiv, xtop, xown, root_class, slice(0, 4 * B), 0)
    for pair in range(KR // 2):
        from_sibling(xother, pair, rq_recv)
    for t in range(4):
        for buffer, first in ((xside, 8 * half), (xother, 8 - 8 * half)):
            product = dot_nn(xown[t * B:(t + 1) * B, :], buffer[...])
            for s in range(8):
                rest[t, first + s] = rtile[first + s, t].astype(F32) - product[:, s * B:(s + 1) * B]

    for n in range(2):
        Starter().landed(came_out.at[n, :, pl.ds(0, 4 * B)], u_recv.at[0, n])
        Starter().landed(came_out.at[n, :, pl.ds(4 * B, 3 * B)], u_recv.at[1, n])
    traffic.drain()
    for store in [keep_store] + panels_stores:
        store.wait()


def main_step(fronts, roots, child_pivots, root_pivots):
    dma = pltpu.SemaphoreType.DMA
    anywhere = pl.BlockSpec(memory_space=pltpu.HBM)
    return pl.pallas_call(
        main_kernel,
        out_shape=[
            pltpu.VMEM((4 * B, KC * B), BF),
            pltpu.VMEM((4 * B, KR * B), BF),
            pltpu.VMEM((4, RS, B, B), F32),
            pltpu.VMEM((2, B, CS * B), BF),
            pltpu.VMEM((2, B, CS * B), BF),
        ],
        in_specs=[anywhere] * 4,
        out_specs=[pl.BlockSpec(memory_space=pltpu.VMEM)] * 5,
        scratch_shapes=[
            pltpu.VMEM((4, B, 8, B), BF),
            pltpu.VMEM((4, B, RS, B), BF),
            pltpu.VMEM((4, B * 8, B), F32),
            pltpu.VMEM((4, B * RS, B), F32),
            pltpu.VMEM((8, 4, B, B), BF),
            pltpu.VMEM((RS, 4, B, B), BF),
            pltpu.VMEM((KC, B, B), F32),
            pltpu.VMEM((KR, B, B), F32),
            pltpu.VMEM((KC, KC // 2 + 1, B, B), BF),
            pltpu.VMEM((KC, 4 * B, B), BF),
            pltpu.VMEM((KC, B, 4 * B), BF),
            pltpu.VMEM((KR, KR // 2 + 1, B, B), BF),
            pltpu.VMEM((KR, 4 * B, B), BF),
            pltpu.VMEM((KR, B, 8 * B), BF),
            pltpu.VMEM((B, 4 * B), BF),
            pltpu.VMEM((B, 8 * B), BF),
            pltpu.VMEM((KC * B, KC * B), BF),
            pltpu.VMEM((4 * B, KC * B), BF),
            pltpu.VMEM((KC * B, 4 * B), BF),
            pltpu.VMEM((KC * B, 4 * B), BF),
            pltpu.VMEM((KR * B, KR * B), BF),
            pltpu.VMEM((KR * B, 8 * B), BF),
            pltpu.VMEM((KR * B, 8 * B), BF),
            pltpu.VMEM((4, B, CS * B), BF),
            dma((4,)), dma((12,)),
            dma((2, 7)), dma((KC,)), dma((1, 7)), dma((KR,)),
            dma((2, 8)), dma((2, KC)), dma((1, 8)), dma((2, KR)),
            dma((64,)), dma((2, KC)), dma((64,)), dma((1, KC)),
            dma((64,)), dma((KR,)), dma((64,)), dma((KR,)),
            dma((2, 2)), dma((2, 2)), dma((5,)), dma((5,)), dma((2,)), dma((2,)),
        ],
        compiler_params=pltpu.CompilerParams(
            collective_id=0, has_side_effects=True, vmem_limit_bytes=56 * 2**20
        ),
        cost_estimate=pl.CostEstimate(flops=10**10, bytes_accessed=10**7, transcendentals=0),
    )(fronts, roots, child_pivots, root_pivots)


def add_kernel(maps, rest, keep, came, panels, root_panels, out, panels_out, root_panels_out, total, wide, done, sems):
    child, half, row, col = position()
    passes = [
        pltpu.make_async_copy(panels, panels_out, sems.at[0]),
        pltpu.make_async_copy(root_panels, root_panels_out, sems.at[1]),
    ]
    for copy in passes:
        copy.start()
    for t in range(4):
        total[t] = rest[t]
    for source, tiles in ((child, keep), (1 - child, came)):
        for p in range(2):
            i = (2 * p + child) * 16 + half * 8 + row - KC
            for n in range(7):
                s = 1 + 3 * half + n if n < 4 else 1 - 4 * half + n
                j = s * 8 + col - KC

                @pl.when((i >= 0) & (j >= 0))
                def _():
                    below = maps[source, jnp.maximum(i, 0)] // 32
                    across = maps[source, jnp.maximum(j, 0)] // 8
                    tile = tiles[p, :, n * B:(n + 1) * B].astype(F32)
                    total[below, across] = total[below, across] + tile
    stores = []
    for t in range(4):
        for s in range(RS):
            wide[t, pl.ds(s, B, stride=RS), :] = total[t, s]
        for b in range(0, B, 32):
            done[t, b:b + 32] = wide[t, b * RS:(b + 32) * RS, :].astype(BF).reshape(32, RS, B)
        stores.append(pltpu.make_async_copy(done.at[t], out.at[t], sems.at[2 + t]))
        stores[-1].start()
    for copy in stores + passes:
        copy.wait()


def add_step(maps, rest, keep, came, panels, root_panels):
    anywhere = pl.BlockSpec(memory_space=pltpu.HBM)
    return pl.pallas_call(
        add_kernel,
        out_shape=[
            jax.ShapeDtypeStruct((4, B, RS, B), BF),
            jax.ShapeDtypeStruct((4 * B, KC * B), BF),
            jax.ShapeDtypeStruct((4 * B, KR * B), BF),
        ],
        in_specs=[pl.BlockSpec(memory_space=pltpu.SMEM)] + [pl.BlockSpec(memory_space=pltpu.VMEM)] * 5,
        out_specs=[anywhere] * 3,
        scratch_shapes=[
            pltpu.VMEM((4, RS, B, B), F32),
            pltpu.VMEM((4, B * RS, B), F32),
            pltpu.VMEM((4, B, RS, B), BF),
            pltpu.SemaphoreType.DMA((6,)),
        ],
        compiler_params=pltpu.CompilerParams(vmem_limit_bytes=24 * 2**20),
    )(maps, rest, keep, came, panels, root_panels)


def on_device(child_fronts, root_front, child_pivots, root_pivots, child_maps):
    fronts = child_fronts.reshape(4, B, 8, B)
    roots = root_front.reshape(4, B, RS, B)
    panels, root_panels, rest, keep, came = main_step(fronts, roots, child_pivots, root_pivots)
    root_rest, panels, root_panels = add_step(child_maps, rest, keep, came, panels, root_panels)
    return (
        panels.reshape(4, 1, B, KC * B),
        root_panels.reshape(4, 1, B, KR * B),
        root_rest.reshape(4, 1, B, RS, 1, B),
    )


def solution(mesh):
    placed = (
        P(None, ("cube", "row"), None, None, "col", None),
        P(None, ("cube", "row"), None, None, "col", None),
        P(),
        P(),
        P(),
    )
    return jax.shard_map(
        on_device,
        mesh=mesh,
        in_specs=placed,
        out_specs=(
            P(None, ("cube", "row"), None, None),
            P(None, ("cube", "row"), None, None),
            P(None, ("cube", "row"), None, None, "col", None),
        ),
        check_vma=False,
    )
```

```python
import functools

import jax
import jax.numpy as jnp
from jax import lax
from jax.experimental import pallas as pl
from jax.experimental.pallas import tpu as pltpu
from jax.sharding import PartitionSpec as P

B = 128
KC = 10
KR = 4
CS = 7
RS = 16
MESH = pl.DeviceIdType.MESH
BF = jnp.bfloat16
F32 = jnp.float32


def dot_nn(left, right):
    return lax.dot_general(left, right, (((1,), (0,)), ((), ())), preferred_element_type=F32)


def dot_nt(left, right):
    return lax.dot_general(left, right, (((1,), (1,)), ((), ())), preferred_element_type=F32)


def split(value):
    high = value.astype(BF)
    return high, (value - high.astype(F32)).astype(BF)


def times_pivot(value, pivot):
    pivot_high, pivot_low = split(pivot)
    upper = jnp.concatenate([pivot_high, pivot_low], axis=1)
    lower = jnp.concatenate([pivot_high, jnp.zeros_like(pivot_low)], axis=1)
    product = dot_nn(jnp.concatenate(split(value), axis=1), jnp.concatenate([upper, lower], axis=0))
    return product[:, :B] + product[:, B:]


def pivot_times(pivot_t, value):
    pivot_high, pivot_low = split(pivot_t)
    upper = jnp.concatenate([pivot_high, pivot_high], axis=1)
    lower = jnp.concatenate([pivot_low, jnp.zeros_like(pivot_low)], axis=1)
    product = dot_nn(jnp.concatenate([upper, lower], axis=0), jnp.concatenate(split(value), axis=0))
    return product[:B] + product[B:]


def position():
    cube = lax.axis_index("cube")
    return cube // 2, cube % 2, lax.axis_index("row"), lax.axis_index("col")


class Starter:
    def __init__(self, number=0):
        self.number = number

    def send(self, source, target, send_sem, recv_sem, device):
        remote(source, target, send_sem, recv_sem, device).start()

    def landed(self, block, recv_sem):
        child, half, row, col = position()
        remote(block, block, recv_sem, recv_sem, (child * 2 + 1 - half, row, col)).wait_recv()


class Drainer:
    def __init__(self, number=0):
        self.number = number

    def send(self, source, target, send_sem, recv_sem, device):
        remote(source, target, send_sem, recv_sem, device).wait_send()

    def landed(self, block, recv_sem):
        pass


def remote(source, target, send_sem, recv_sem, device):
    return pltpu.make_async_remote_copy(
        src_ref=source, dst_ref=target, send_sem=send_sem, recv_sem=recv_sem,
        device_id=device, device_id_type=MESH,
    )


class Traffic:
    def __init__(self):
        self.pending = []

    def starter(self):
        return Starter()

    def run(self, cond, body, number=0):
        op = Starter(number)
        pl.when(cond)(lambda: body(op))
        self.pending.append((cond, body, number))
        return op.number

    def drain(self):
        for cond, body, number in self.pending:
            pl.when(cond)(lambda: body(Drainer(number)))
        self.pending = []


class PairSpread:
    def __init__(self, traffic, buffer, size, hand, recv, sems):
        self.traffic, self.buffer, self.size, self.hand = traffic, buffer, size, hand
        self.recv, self.sems, self.number = recv, sems, 0
        child, half, row, col = position()
        self.half, self.row, self.x, self.y = half, row, row // 2, row % 2
        self.sibling = (child * 2 + 1 - half, row, col)
        self.plus, self.minus = [(child * 2 + half, (self.x + d) % 4 * 2 + self.y, col) for d in (1, 3)]
        self.across = (child * 2 + half, row + 1 - 2 * self.y, col)
        self.mine = half * 8 + row
        self.other = (1 - half) * 8 + row

    def part(self, slot, half):
        if self.size is None:
            return self.buffer.at[slot], self.recv.at[0, slot]
        start = pl.multiple_of(half * self.size, self.size)
        return self.buffer.at[slot, pl.ds(start, self.size)], self.recv.at[half, slot]

    def _send(self, op, slot, device, half=None):
        block, recv = self.part(slot, self.half if half is None else half)
        op.send(block, block, self.sems.at[op.number], recv, device)
        op.number += 1

    def _wait(self, op, slot, half=None):
        block, recv = self.part(slot, self.half if half is None else half)
        op.landed(block, recv)

    def _pass(self, op, slot):
        if self.size is not None:
            self._send(op, slot, self.sibling)

    def _run(self, cond, body):
        self.number = self.traffic.run(cond, body, self.number)

    def _each(self, chips, body):
        for chip in chips:
            body(chip)
            pl.when(chip < 2)(lambda: body(8 + chip % 2))

    def _row(self, d, e):
        return (self.x + d) % 4 * 2 + (self.y + e) % 2

    def begin(self):
        def own(op):
            slot = self.mine % KC
            if self.size is None:
                block, recv = self.part(slot, self.half)
                op.send(self.hand, block, self.sems.at[op.number], recv, self.sibling)
                op.number += 1
            else:
                self._send(op, slot, self.sibling, 1 - self.half)
            for device in (self.across, self.plus, self.minus):
                self._send(op, slot, device)
            self._pass(op, slot)

        def others(op):
            slot = self.other % KC
            self._wait(op, slot)
            for device in (self.across, self.plus, self.minus):
                self._send(op, slot, device)

        self._run(self.mine < KC, own)
        self._run(self.other < KC, others)

    def _onward(self, op, slot, d):
        if d == 3:
            pl.when(slot < 4)(lambda: self._send(op, slot, self.plus))
        else:
            pl.when(slot >= 4)(lambda: self._send(op, slot, self.minus))

    def relay(self):
        def first(op):
            for d in (3, 1):
                def body(slot):
                    self._wait(op, slot)
                    self._onward(op, slot, d)
                    self._send(op, slot, self.across)
                    self._pass(op, slot)

                self._each([self._row(d, 0)], body)

        def second(op):
            def body(slot):
                self._wait(op, slot)
                self._send(op, slot, self.plus)
                self._send(op, slot, self.minus)
                self._pass(op, slot)

            self._each([self._row(0, 1)], body)

        self._run(self.half == 0, first)
        self._run(self.half == 1, second)

    def relay2(self):
        def first(op):
            def body(slot):
                self._wait(op, slot)
                self._send(op, slot, self.across)
                self._pass(op, slot)

            self._each([self._row(2, 0)], body)

        def second(op):
            for e in range(2):
                for d in (3, 1):
                    def body(slot):
                        self._wait(op, slot)
                        self._onward(op, slot, d)
                        self._pass(op, slot)

                    self._each([self._row(d, e)], body)

        self._run(self.half == 0, first)
        self._run(self.half == 1, second)

    def settle(self):
        def body(op, slot):
            self._wait(op, slot)
            self._pass(op, slot)

        def first(op):
            self._each([self._row(d, 1) for d in (0, 3, 1, 2)], lambda slot: body(op, slot))

        def second(op):
            self._each([self._row(2, e) for e in range(2)], lambda slot: body(op, slot))

        self._run(self.half == 0, first)
        self._run(self.half == 1, second)

    def finish(self):
        if self.size is None:
            return
        op = self.traffic.starter()
        pl.when(self.other < KC)(lambda: self._wait(op, self.other % KC, 1 - self.half))
        chips = [self._row(d, e) for d in range(4) for e in range(2)][1:]
        self._each(chips, lambda slot: self._wait(op, slot, 1 - self.half))


class PlaneShare:
    def __init__(self, traffic, buffer, hand, recv, sems):
        self.traffic, self.buffer, self.hand, self.recv, self.sems, self.number = traffic, buffer, hand, recv, sems, 0
        child, half, row, col = position()
        self.half = half
        self.sibling = (child * 2 + 1 - half, row, col)
        x, y = row // 2, child * 2 + row % 2

        def device(dx, dy):
            place = (y + dy) % 4
            return (place // 2 * 2 + half, (x + dx) % 4 * 2 + place % 2, col)

        def either(first, second):
            return tuple(jnp.where(half == 0, one, two) for one, two in zip(first, second))

        self.first = [either(device(d, 0), device(0, d)) for d in (1, 3)]
        self.second = [either(device(0, d), device(d, 0)) for d in (1, 3)]
        self.slots = []
        for i in range(KR):
            begin_1 = jnp.where(half == 0, i // 2, i % 2)
            begin_2 = jnp.where(half == 0, i % 2, i // 2)
            far_1 = (jnp.where(half == 0, x, y) - begin_1 + 4) % 4
            far_2 = (jnp.where(half == 0, y, x) - begin_2 + 4) % 4
            self.slots.append((i, begin_1, begin_2, far_1, far_2))

    def _send(self, op, i, device):
        block = self.buffer.at[i]
        op.send(block, block, self.sems.at[op.number], self.recv.at[i], device)
        op.number += 1

    def _wait(self, op, i):
        op.landed(self.buffer.at[i], self.recv.at[i])

    def _run(self, cond, body):
        self.number = self.traffic.run(cond, body, self.number)

    def _onward(self, op, i, begin, far, devices):
        pl.when((begin == 1) & (far == 1))(lambda: self._send(op, i, devices[0]))
        pl.when((begin == 0) & (far == 3))(lambda: self._send(op, i, devices[1]))

    def begin(self):
        for i, begin_1, begin_2, far_1, far_2 in self.slots:
            chip = (far_1 == 0) & (far_2 == 0)

            def body(op, i=i):
                @pl.when(self.half == 0)
                def _():
                    hand = self.buffer.at[i] if self.hand is None else self.hand
                    op.send(hand, self.buffer.at[i], self.sems.at[op.number], self.recv.at[i], self.sibling)

                op.number += 1
                pl.when(self.half == 1)(lambda: self._wait(op, i))
                for device in self.first + self.second:
                    self._send(op, i, device)

            self._run(chip, body)

    def relay(self):
        for i, begin_1, begin_2, far_1, far_2 in self.slots:
            def body(op, i=i, begin_1=begin_1, far_1=far_1):
                self._wait(op, i)
                self._onward(op, i, begin_1, far_1, self.first)
                for device in self.second:
                    self._send(op, i, device)

            self._run((far_2 == 0) & (far_1 % 2 == 1), body)

    def relay2(self):
        for i, begin_1, begin_2, far_1, far_2 in self.slots:
            def body(op, i=i):
                self._wait(op, i)
                for device in self.second:
                    self._send(op, i, device)

            self._run((far_2 == 0) & (far_1 == 2), body)

    def relay3(self):
        for i, begin_1, begin_2, far_1, far_2 in self.slots:
            def body(op, i=i, begin_2=begin_2, far_2=far_2):
                self._wait(op, i)
                self._onward(op, i, begin_2, far_2, self.second)

            self._run(far_2 % 2 == 1, body)

    def finish(self):
        op = self.traffic.starter()
        for i, begin_1, begin_2, far_1, far_2 in self.slots:
            pl.when(far_2 == 2)(lambda: self._wait(op, i))


class Line:
    def __init__(self, traffic, buffer, count, recv, sems):
        self.traffic, self.buffer, self.count, self.recv, self.sems = traffic, buffer, count, recv, sems
        child, half, row, col = position()
        self.col = col
        self.places = [(child * 2 + half, row, (col + d) % 8) for d in (1, 7)]

    def _each(self, step, body):
        base = (self.col + step + 8) % 8
        for extra in range((self.count + 7) // 8):
            limit = min(self.count - 8 * extra, 8)

            def run(op, extra=extra, limit=limit):
                body(op, extra, 8 * extra + base % limit)

            self.traffic.run(base < limit, run)

    def begin(self):
        def body(op, extra, slot):
            block = self.buffer.at[slot]
            for way in range(2):
                op.send(block, block, self.sems.at[extra, way], self.recv.at[0, slot], self.places[way])

        self._each(0, body)

    def relay(self, step):
        for way in range(2):
            def body(op, extra, slot, way=way):
                block = self.buffer.at[slot]
                op.landed(block, self.recv.at[0, slot])
                number = 0
                if step == 3:
                    block = self.buffer.at[slot, pl.ds(way * 2 * B, 2 * B)]
                    number = way
                op.send(
                    block, block, self.sems.at[extra, 2 * step + way], self.recv.at[number, slot], self.places[way]
                )

            self._each(step if way else -step, body)

    def finish(self):
        def body(op, extra, slot):
            for way in range(2):
                op.landed(self.buffer.at[slot, pl.ds(way * 2 * B, 2 * B)], self.recv.at[way, slot])

        self._each(4, body)


class TopLine:
    def __init__(self, traffic, count, buffer, recv, sems, owns, mine):
        child, half, row, col = position()
        self.traffic, self.count, self.buffer, self.recv, self.sems = traffic, count, buffer, recv, sems
        self.owns, self.mine, self.col = owns, mine % count, col
        self.depth = count // 2 + 1
        self.places = [(child * 2 + half, row, (col + d) % 8) for d in (1, 7, 2, 6, 3, 5, 4)]

    def held(self):
        for extra in range((self.count + 7) // 8):
            limit = min(self.count - 8 * extra, 8)
            index = 8 * extra + self.col % limit
            place = (index - self.mine + self.count) % self.count
            yield extra, self.owns & (self.col < limit) & (place < self.depth), index, place % self.depth

    def begin(self):
        for extra, cond, index, place in self.held():
            def body(op, extra=extra, index=index, place=place):
                block = self.buffer.at[self.mine, place]
                for n, device in enumerate(self.places):
                    op.send(block, block, self.sems.at[extra, n], self.recv.at[index], device)

            self.traffic.run(cond, body)

    def finish(self):
        op = self.traffic.starter()

        @pl.when(self.owns)
        def _():
            for place in range(self.depth):
                index = (self.mine + place) % self.count

                @pl.when(index % 8 != self.col)
                def _():
                    op.landed(self.buffer.at[self.mine, place], self.recv.at[index])


def greet_all():
    child, half, row, col = position()
    cube = child * 2 + half
    x, y = row // 2, child * 2 + row % 2
    barrier = pltpu.get_barrier_semaphore()
    others = [(cube, row, (col + d) % 8) for d in range(1, 8)]
    others += [(cube, (x + d) % 4 * 2 + row % 2, col) for d in range(1, 4)]
    others += [((y + d) % 4 // 2 * 2 + half, x * 2 + (y + d) % 2, col) for d in range(1, 4)]
    others += [(child * 2 + 1 - half, row, col)]
    for device in others:
        pl.semaphore_signal(barrier, inc=1, device_id=device, device_id_type=MESH)
    return barrier, len(others)


def top_tile(count, top, i, k):
    place = (k - i) % count
    if place <= count // 2:
        return top[i, place].astype(F32)
    return top[k, (i - k) % count].astype(F32).T


def factor_top(count, pair, top, pivots, panels):
    k = 2 * pair
    at = k * B
    first = jnp.concatenate([top_tile(count, top, i, k) for i in range(k, count)], axis=0)
    second = jnp.concatenate([top_tile(count, top, i, k + 1) for i in range(k + 1, count)], axis=0)
    if pair:
        both = dot_nt(panels[at:, :at], panels[at:at + 2 * B, :at])
        first = first - both[:, :B]
        second = second - both[B:, B:]
    first = times_pivot(first, pivots[k]).astype(BF)
    panels[at:, at:at + B] = first
    second = second - dot_nt(first[B:], first[B:2 * B])
    panels[at + B:, at + B:at + 2 * B] = times_pivot(second, pivots[k + 1]).astype(BF)


def factor_own(pair, down, pivots, panels_top, panels, row_class, rows, first_block):
    k = 2 * pair
    at = k * B
    length = rows.stop - rows.start
    block = (lax.broadcasted_iota(jnp.int32, (length, B), 0) + rows.start) // B
    row_block = block == first_block
    first = down[k, rows].astype(F32)
    second = down[k + 1, rows].astype(F32)
    if pair:
        both = dot_nt(panels[rows, :at], panels_top[at:at + 2 * B, :at])
        first = first - both[:, :B]
        second = second - both[:, B:]
    first = times_pivot(first, pivots[k])
    first = jnp.where(row_block & (row_class < k), 0.0, first).astype(BF)
    panels[rows, at:at + B] = first
    second = second - dot_nt(first, panels_top[at + B:at + 2 * B, at:at + B])
    second = times_pivot(second, pivots[k + 1])
    second = jnp.where(row_block & (row_class < k + 1), 0.0, second).astype(BF)
    panels[rows, at + B:at + 2 * B] = second


def factor_wide(pair, side, pivots, panels_top, wide, first_tile):
    k = 2 * pair
    at = k * B
    col_block = lax.broadcasted_iota(jnp.int32, (B, wide.shape[1]), 1) < B
    first = side[k].astype(F32)
    second = side[k + 1].astype(F32)
    if pair:
        both = dot_nn(panels_top[at:at + 2 * B, :at], wide[:at, :])
        first = first - both[:B]
        second = second - both[B:]
    first = pivot_times(pivots[k].T, first)
    first = jnp.where(col_block & (first_tile < k), 0.0, first).astype(BF)
    wide[at:at + B, :] = first
    second = second - dot_nn(panels_top[at + B:at + 2 * B, at:at + B], first)
    second = pivot_times(pivots[k + 1].T, second)
    second = jnp.where(col_block & (first_tile < k + 1), 0.0, second).astype(BF)
    wide[at + B:at + 2 * B, :] = second


def main_kernel(
    fronts, roots, child_pivots, root_pivots,
    panels_out, xown, rest, keep_out, came_out,
    craw, rraw, cwide, rwide, ctile, rtile, cpiv, rpiv,
    top, down, side, rtop, rdown, rside,
    hand, rhand, ctop, cown, cside, cother, xtop, xside, xother, update,
    load_sem, store_sem, tl_send, tl_recv, rtl_send, rtl_recv, line_send, line_recv, rline_send, rline_recv,
    t_send, t_recv, s_send, s_recv, rt_send, rt_recv, rs_send, rs_recv, u_send, u_recv,
    q_send, q_recv, rq_send, rq_recv,
):
    child, half, row, col = position()
    mine = half * 8 + row
    root_class = child * 16 + mine
    owns = mine < KC
    root_owns = (child == 0) & (half == 0) & (row < KR)

    loads = [
        pltpu.make_async_copy(fronts, craw, load_sem.at[0]),
        pltpu.make_async_copy(child_pivots.at[child], cpiv, load_sem.at[1]),
        pltpu.make_async_copy(roots, rraw, load_sem.at[2]),
        pltpu.make_async_copy(root_pivots, rpiv, load_sem.at[3]),
    ]
    for load in loads:
        load.start()
    barrier, count = greet_all()

    traffic = Traffic()
    top_line = TopLine(traffic, KC, top, tl_recv, tl_send, owns, mine)
    root_top_line = TopLine(traffic, KR, rtop, rtl_recv, rtl_send, root_owns, row)
    line = Line(traffic, down, KC, line_recv, line_send)
    root_line = Line(traffic, rdown, KR, rline_recv, rline_send)
    top_spread = PairSpread(traffic, top, 3, None, t_recv, t_send)
    side_spread = PairSpread(traffic, side, None, hand, s_recv, s_send)
    root_top_spread = PlaneShare(traffic, rtop, None, rt_recv, rt_send)
    root_side_spread = PlaneShare(traffic, rside, rhand, rs_recv, rs_send)
    always = col >= 0

    order = [1 - child, 3 - child, child, 2 + child]
    own_first = 1 + 3 * half
    other_first = 5 - 4 * half

    def part_tiles(raw, wide, tiles, t):
        stride = raw.shape[2]
        for b in range(0, B, 32):
            at = b * stride
            wide[at:at + 32 * stride, :] = raw[t, b:b + 32].astype(F32).reshape(32 * stride, B)
        for s in range(stride):
            tiles[s, t] = wide[pl.ds(s, B, stride=stride), :].astype(BF)

    def place_top(line_top, tiles):
        for extra, cond, index, place in line_top.held():
            @pl.when(cond)
            def _():
                line_top.buffer[line_top.mine, place] = tiles[extra, 0]

    def place_columns(line_buffer, count, line_top, tiles, order):
        for extra, cond, index, place in line_top.held():
            @pl.when((col + 8 * extra) < count)
            def _():
                for n, t in enumerate(order):
                    line_buffer[index, n * B:(n + 1) * B] = tiles[extra, t]

    loads[0].wait()
    part_tiles(craw, cwide.at[0], ctile, 0)
    place_top(top_line, ctile)
    pl.semaphore_wait(barrier, count)
    top_line.begin()
    for t in range(1, 4):
        part_tiles(craw, cwide.at[t], ctile, t)
    place_columns(down, KC, top_line, ctile, order)
    line.begin()

    @pl.when(owns)
    def _():
        for s in range(4):
            columns = slice(s * B, (s + 1) * B)
            side[mine % KC, :, columns] = ctile[own_first + s, 0]
            hand[:, columns] = ctile[4 - 3 * half + s, 0]

    side_spread.begin()
    loads[2].wait()
    for t in range(4):
        part_tiles(rraw, rwide.at[t], rtile, t)
    place_top(root_top_line, rtile)
    place_columns(rdown, KR, root_top_line, rtile, range(4))

    @pl.when(root_owns)
    def _():
        for s in range(8):
            columns = slice(s * B, (s + 1) * B)
            rside[row % KR, :, columns] = rtile[s, 0]
            rhand[:, columns] = rtile[8 + s, 0]

    root_top_line.begin()
    top_line.finish()
    top_spread.begin()
    line.relay(1)
    top_spread.relay()
    side_spread.relay()
    line.relay(2)
    top_spread.relay2()
    root_top_line.finish()
    root_top_spread.begin()
    root_side_spread.begin()
    side_spread.relay2()
    top_spread.settle()
    line.relay(3)
    root_line.begin()
    top_spread.finish()

    loads[1].wait()
    loads[3].wait()
    for pair in range(2):
        factor_top(KC, pair, top, cpiv, ctop)
    root_top_spread.relay()
    root_side_spread.relay()
    for pair in range(2, 4):
        factor_top(KC, pair, top, cpiv, ctop)
    root_top_spread.relay2()
    root_side_spread.relay2()
    root_line.relay(1)
    factor_top(KC, 4, top, cpiv, ctop)
    line.finish()
    side_spread.settle()

    sibling = (child * 2 + 1 - half, row, col)
    partner = ((1 - child) * 2 + half, row, col)
    first_block = jnp.where(child == 1, 0, 2)

    def to_sibling(buffer, other, pair, send_sem, recv_sem):
        block = pl.ds(2 * pair * B, 2 * B)

        def body(op):
            op.send(buffer.at[block], other.at[block], send_sem.at[pair], recv_sem.at[pair], sibling)

        traffic.run(always, body)

    def from_sibling(other, pair, recv_sem):
        Starter().landed(other.at[pl.ds(2 * pair * B, 2 * B)], recv_sem.at[pair])

    def update_own(n):
        product = dot_nn(cown[n * B:(n + 1) * B, :], cside[...])
        for s in range(4):
            value = ctile[own_first + s, order[n]].astype(F32)
            update[n, :, s * B:(s + 1) * B] = (value - product[:, s * B:(s + 1) * B]).astype(BF)

    def update_other(n):
        columns = pl.ds(pl.multiple_of((1 - half) * B, B), 3 * B)
        product = dot_nn(cown[n * B:(n + 1) * B, :], cother[:, columns])
        for s in range(3):
            value = ctile[other_first + s, order[n]].astype(F32)
            update[n, :, (4 + s) * B:(5 + s) * B] = (value - product[:, s * B:(s + 1) * B]).astype(BF)

    def send_update(n, part):
        columns = pl.ds(0, 4 * B) if part == 0 else pl.ds(4 * B, 3 * B)

        def body(op):
            op.send(
                update.at[n, :, columns], came_out.at[n, :, columns],
                u_send.at[part, n], u_recv.at[part, n], partner,
            )

        traffic.run(always, body)

    for pair in range(KC // 2):
        factor_wide(pair, side, cpiv, ctop, cside, 8 + 24 * half + col)
        factor_own(pair, down, cpiv, ctop, cown, mine, slice(0, 2 * B), first_block)
        to_sibling(cside, cother, pair, q_send, q_recv)
    root_top_spread.relay3()
    root_side_spread.relay3()
    for n in range(2):
        update_own(n)
        send_update(n, 0)
    for pair in range(KC // 2):
        from_sibling(cother, pair, q_recv)
    for n in range(2):
        update_other(n)
        send_update(n, 1)
    root_line.relay(2)
    for pair in range(KC // 2):
        factor_own(pair, down, cpiv, ctop, cown, mine, slice(2 * B, 4 * B), first_block)
    panels_stores = []
    for n in range(4):
        rows = pl.ds(pl.multiple_of(order[n] * B, B), B)
        panels_stores.append(
            pltpu.make_async_copy(cown.at[pl.ds(n * B, B)], panels_out.at[rows], store_sem.at[8 + n])
        )
        panels_stores[-1].start()
    for n in range(2, 4):
        update_own(n)
        update_other(n)
    keep_store = pltpu.make_async_copy(update.at[pl.ds(2, 2)], keep_out, store_sem.at[0])
    keep_store.start()
    root_line.relay(3)

    root_top_spread.finish()
    for pair in range(KR // 2):
        factor_top(KR, pair, rtop, rpiv, xtop)
    root_side_spread.finish()
    for pair in range(KR // 2):
        factor_wide(pair, rside, rpiv, xtop, xside, 64 * half + col)
        to_sibling(xside, xother, pair, rq_send, rq_recv)
    root_line.finish()
    for pair in range(KR // 2):
        factor_own(pair, rdown, rpiv, xtop, xown, root_class, slice(0, 4 * B), 0)
    for pair in range(KR // 2):
        from_sibling(xother, pair, rq_recv)
    for t in range(4):
        for buffer, first in ((xside, 8 * half), (xother, 8 - 8 * half)):
            product = dot_nn(xown[t * B:(t + 1) * B, :], buffer[...])
            for s in range(8):
                rest[t, first + s] = rtile[first + s, t].astype(F32) - product[:, s * B:(s + 1) * B]

    traffic.drain()
    for n in range(2):
        Starter().landed(came_out.at[n, :, pl.ds(0, 4 * B)], u_recv.at[0, n])
        Starter().landed(came_out.at[n, :, pl.ds(4 * B, 3 * B)], u_recv.at[1, n])
    for store in [keep_store] + panels_stores:
        store.wait()


def main_step(fronts, roots, child_pivots, root_pivots):
    dma = pltpu.SemaphoreType.DMA
    anywhere = pl.BlockSpec(memory_space=pltpu.HBM)
    return pl.pallas_call(
        main_kernel,
        out_shape=[
            pltpu.VMEM((4 * B, KC * B), BF),
            pltpu.VMEM((4 * B, KR * B), BF),
            pltpu.VMEM((4, RS, B, B), F32),
            pltpu.VMEM((2, B, CS * B), BF),
            pltpu.VMEM((2, B, CS * B), BF),
        ],
        in_specs=[anywhere] * 4,
        out_specs=[pl.BlockSpec(memory_space=pltpu.VMEM)] * 5,
        scratch_shapes=[
            pltpu.VMEM((4, B, 8, B), BF),
            pltpu.VMEM((4, B, RS, B), BF),
            pltpu.VMEM((4, B * 8, B), F32),
            pltpu.VMEM((4, B * RS, B), F32),
            pltpu.VMEM((8, 4, B, B), BF),
            pltpu.VMEM((RS, 4, B, B), BF),
            pltpu.VMEM((KC, B, B), F32),
            pltpu.VMEM((KR, B, B), F32),
            pltpu.VMEM((KC, KC // 2 + 1, B, B), BF),
            pltpu.VMEM((KC, 4 * B, B), BF),
            pltpu.VMEM((KC, B, 4 * B), BF),
            pltpu.VMEM((KR, KR // 2 + 1, B, B), BF),
            pltpu.VMEM((KR, 4 * B, B), BF),
            pltpu.VMEM((KR, B, 8 * B), BF),
            pltpu.VMEM((B, 4 * B), BF),
            pltpu.VMEM((B, 8 * B), BF),
            pltpu.VMEM((KC * B, KC * B), BF),
            pltpu.VMEM((4 * B, KC * B), BF),
            pltpu.VMEM((KC * B, 4 * B), BF),
            pltpu.VMEM((KC * B, 4 * B), BF),
            pltpu.VMEM((KR * B, KR * B), BF),
            pltpu.VMEM((KR * B, 8 * B), BF),
            pltpu.VMEM((KR * B, 8 * B), BF),
            pltpu.VMEM((4, B, CS * B), BF),
            dma((4,)), dma((12,)),
            dma((2, 7)), dma((KC,)), dma((1, 7)), dma((KR,)),
            dma((2, 8)), dma((2, KC)), dma((1, 8)), dma((2, KR)),
            dma((64,)), dma((2, KC)), dma((64,)), dma((1, KC)),
            dma((64,)), dma((KR,)), dma((64,)), dma((KR,)),
            dma((2, 2)), dma((2, 2)), dma((5,)), dma((5,)), dma((2,)), dma((2,)),
        ],
        compiler_params=pltpu.CompilerParams(
            collective_id=0, has_side_effects=True, vmem_limit_bytes=56 * 2**20
        ),
        cost_estimate=pl.CostEstimate(flops=10**10, bytes_accessed=10**7, transcendentals=0),
    )(fronts, roots, child_pivots, root_pivots)


def add_kernel(maps, rest, keep, came, panels, root_panels, out, panels_out, root_panels_out, total, wide, done, sems):
    child, half, row, col = position()
    passes = [
        pltpu.make_async_copy(panels, panels_out, sems.at[0]),
        pltpu.make_async_copy(root_panels, root_panels_out, sems.at[1]),
    ]
    for copy in passes:
        copy.start()
    for t in range(4):
        total[t] = rest[t]
    for source, tiles in ((child, keep), (1 - child, came)):
        for p in range(2):
            i = (2 * p + child) * 16 + half * 8 + row - KC
            for n in range(7):
                s = 1 + 3 * half + n if n < 4 else 1 - 4 * half + n
                j = s * 8 + col - KC

                @pl.when((i >= 0) & (j >= 0))
                def _():
                    below = maps[source, jnp.maximum(i, 0)] // 32
                    across = maps[source, jnp.maximum(j, 0)] // 8
                    tile = tiles[p, :, n * B:(n + 1) * B].astype(F32)
                    total[below, across] = total[below, across] + tile
    stores = []
    for t in range(4):
        for s in range(RS):
            wide[t, pl.ds(s, B, stride=RS), :] = total[t, s]
        for b in range(0, B, 32):
            done[t, b:b + 32] = wide[t, b * RS:(b + 32) * RS, :].astype(BF).reshape(32, RS, B)
        stores.append(pltpu.make_async_copy(done.at[t], out.at[t], sems.at[2 + t]))
        stores[-1].start()
    for copy in stores + passes:
        copy.wait()


def add_step(maps, rest, keep, came, panels, root_panels):
    anywhere = pl.BlockSpec(memory_space=pltpu.HBM)
    return pl.pallas_call(
        add_kernel,
        out_shape=[
            jax.ShapeDtypeStruct((4, B, RS, B), BF),
            jax.ShapeDtypeStruct((4 * B, KC * B), BF),
            jax.ShapeDtypeStruct((4 * B, KR * B), BF),
        ],
        in_specs=[pl.BlockSpec(memory_space=pltpu.SMEM)] + [pl.BlockSpec(memory_space=pltpu.VMEM)] * 5,
        out_specs=[anywhere] * 3,
        scratch_shapes=[
            pltpu.VMEM((4, RS, B, B), F32),
            pltpu.VMEM((4, B * RS, B), F32),
            pltpu.VMEM((4, B, RS, B), BF),
            pltpu.SemaphoreType.DMA((6,)),
        ],
        compiler_params=pltpu.CompilerParams(vmem_limit_bytes=24 * 2**20),
    )(maps, rest, keep, came, panels, root_panels)


def on_device(child_fronts, root_front, child_pivots, root_pivots, child_maps):
    fronts = child_fronts.reshape(4, B, 8, B)
    roots = root_front.reshape(4, B, RS, B)
    panels, root_panels, rest, keep, came = main_step(fronts, roots, child_pivots, root_pivots)
    root_rest, panels, root_panels = add_step(child_maps, rest, keep, came, panels, root_panels)
    return (
        panels.reshape(4, 1, B, KC * B),
        root_panels.reshape(4, 1, B, KR * B),
        root_rest.reshape(4, 1, B, RS, 1, B),
    )


def solution(mesh):
    placed = (
        P(None, ("cube", "row"), None, None, "col", None),
        P(None, ("cube", "row"), None, None, "col", None),
        P(),
        P(),
        P(),
    )
    return jax.shard_map(
        on_device,
        mesh=mesh,
        in_specs=placed,
        out_specs=(
            P(None, ("cube", "row"), None, None),
            P(None, ("cube", "row"), None, None),
            P(None, ("cube", "row"), None, None, "col", None),
        ),
        check_vma=False,
    )
```
